256 devices in a mesh: tm: 64 (over z, x, core), head: 4 (over y).
Axes of the slice: x: 4, y: 4, z: 8, core: 2. Of those that a mesh axis runs over, the one named last changes fastest.
Arguments:
- queries: bfloat16 [24576, 1024], P('tm', 'head'), may hold values from -6 to 6
- key_rows: bfloat16 [24576, 1024], P('tm', 'head'), may hold values from -6 to 6
- value_rows: bfloat16 [24576, 1024], P('tm', 'head'), may hold values from -6 to 6
- out_weight: bfloat16 [1024, 1024], P('head'), may hold values from -0.1875 to 0.1875
Outputs:
- layer_out: bfloat16 [24576, 1024], P(('tm', 'head'))
The draws below stay inside these ranges and needn't reach their ends.
All inputs are finite; a program needn't handle non-finite values.
Results may differ from the reference program's by a relative error of at most 0.015.
Values may be sent and summed in bfloat16 or wider, within the bound.
No kernel may reach another device: no remote copies, remote signals or barrier semaphores. Data moves between devices by JAX's collectives and lax.ppermute only.
A program may use at most 128 MiB of HBM per device.

```python
import math
import jax
import jax.numpy as jnp
from jax import lax

D = 1024
HEADS = 16
HEAD_DIM = 64
TOKENS = 24576


def draw_queries(key, part):
    key = jax.random.fold_in(key, 11)
    shape = (TOKENS, HEADS * HEAD_DIM)
    base = jnp.clip(jax.random.normal(key, shape, jnp.float32), -4.0, 4.0)
    return base.astype(jnp.bfloat16)


def draw_key_rows(key, part):
    key = jax.random.fold_in(key, 23)
    shape = (TOKENS, HEADS * HEAD_DIM)
    base = jnp.clip(jax.random.normal(key, shape, jnp.float32), -4.0, 4.0)
    return base.astype(jnp.bfloat16)


def shard_levels(own_key, extent, shards, least, largest):
    loudness = 1.0
    for position, blocks in shards:
        steps = jax.random.uniform(jax.random.fold_in(jax.random.fold_in(own_key, 6), position), (blocks,), jnp.float32, least / len(shards), largest / len(shards))
        loudness = loudness * jnp.repeat(jnp.exp(steps), extent[position] // blocks).reshape((-1,) + (1,) * (len(extent) - 1 - position))
    return loudness


def centred(rng, dims, scale, limit, cuts=(), kind=jnp.bfloat16):
    drawn = jax.random.normal(rng, dims, jnp.float32) * scale
    if len(cuts) > 0:
        drawn = shard_levels(rng, dims, cuts, -0.22, 0.18) * drawn
    return jnp.clip(drawn, min=-limit, max=limit).astype(kind)


def setup_inputs(seed: int = 0) -> dict:
    keys = jax.random.split(jax.random.key(seed), 5)
    return {
        "queries": draw_queries(jax.random.fold_in(keys[4], 71), 0),
        "key_rows": draw_key_rows(jax.random.fold_in(keys[4], 71), 0),
        "value_rows": centred(keys[2], (TOKENS, HEADS * HEAD_DIM), 1.0, 6.0, ((0, 64), (1, 4))),
        "out_weight": centred(keys[3], (HEADS * HEAD_DIM, D), (HEADS * HEAD_DIM) ** -0.5, 0.1875, ((0, 4),)),
    }


def reference(queries, key_rows, value_rows, out_weight):
    width = queries.shape[1]
    rows_block = min(128, TOKENS)
    key_all = key_rows.astype(jnp.float32).reshape(TOKENS, HEADS, HEAD_DIM)
    value_all = value_rows.astype(jnp.float32).reshape(TOKENS, HEADS, HEAD_DIM)
    positions = jnp.arange(TOKENS, dtype=jnp.int32)
    factor = 1.0 / math.sqrt(HEAD_DIM)

    def one_block(index_q):
        offset = (index_q * rows_block).astype(jnp.int32)
        query_block = lax.dynamic_slice_in_dim(queries, offset, rows_block, 0)
        query_block = query_block.astype(jnp.float32).reshape(rows_block, HEADS, HEAD_DIM)
        scores = jnp.einsum('rhd,khd->hrk', query_block, key_all, precision=lax.Precision.HIGHEST) * factor
        query_pos = offset + jnp.arange(rows_block, dtype=jnp.int32)
        causal = query_pos[:, None] >= positions[None, :]
        scores = jnp.where(causal[None], scores, -1e+30)
        top = lax.optimization_barrier(jnp.max(scores, axis=-1, keepdims=True))
        expo = jnp.where(causal[None], jnp.exp(scores - top), 0.0)
        total = lax.optimization_barrier(jnp.sum(expo, axis=-1))
        weights = lax.optimization_barrier(expo.astype(jnp.bfloat16)).astype(jnp.float32)
        mixed = jnp.einsum('hrk,khd->hrd', weights, value_all, precision=lax.Precision.HIGHEST)
        mixed = mixed / total[..., None]
        return jnp.transpose(mixed, (1, 0, 2)).reshape(rows_block, width).astype(jnp.bfloat16)
    mixed_all = lax.map(one_block, jnp.arange(TOKENS // rows_block, dtype=jnp.int32))
    mixed_all = mixed_all.reshape(TOKENS, width)
    return jnp.dot(mixed_all, out_weight, preferred_element_type=jnp.float32).astype(jnp.bfloat16)
```

```python
import functools
import math

import jax
import jax.numpy as jnp
import numpy as np
from jax import lax
from jax.experimental import pallas as pl
from jax.experimental.pallas import tpu as pltpu
from jax.sharding import Mesh, PartitionSpec as P

HEAD_DIM = 64
F32 = jnp.float32
BF16 = jnp.bfloat16
MATMUL = (((1,), (0,)), ((), ()))

NZ, NX, NC, NY = 8, 4, 2, 4
CHUNK = 384
PIECE = CHUNK // NZ
COLS = NZ * NX * PIECE
QB = 2 * NX * PIECE
KEYS = NX * NC * CHUNK
SPAN = NC * CHUNK
VROWS = 80
LIMIT = 90.0


def query_offsets():
    n = np.arange(COLS)
    p, j = n // PIECE, n % PIECE
    main = j < 32
    group = np.where(main, j // 8, (j - 32) // 4)
    row = np.where(main, j % 8, 8 + (j - 32) % 4)
    return (SPAN * p + 96 * group + row).astype(np.int32)


def prepare_queries(q_ref, o_ref):
    q = q_ref[...].astype(F32) * (math.log2(math.e) / math.sqrt(HEAD_DIM))
    high = q.astype(BF16).astype(F32)
    both = jnp.concatenate([high, q - high], axis=1)
    o_ref[...] = both.T.astype(BF16)


def load_keys(kv, k2, vt, kmax):
    keys, values = kv[:, :HEAD_DIM], kv[:, HEAD_DIM:]
    twice = jnp.concatenate([keys, keys], axis=1)
    k2[...] = twice
    vt[:HEAD_DIM, :] = values.T
    largest = jnp.max(jnp.abs(twice.astype(F32)).reshape(KEYS // 8, 8, 128), axis=0)
    kmax[...] = jnp.maximum(kmax[...], largest)


def kept(s, base, qpos):
    seg = lax.broadcasted_iota(jnp.int32, (CHUNK, qpos.shape[1]), 0)
    return seg <= qpos - base


def fast_blocks(zk, q2, qpos, k2, vt, acc):
    def body(b, carry):
        cols = pl.ds(pl.multiple_of(b * QB, QB), QB)
        qb = q2[:, cols]
        at = qpos[:, cols] - zk * KEYS
        total = acc[:, cols]
        for half in range(NC):
            rows = pl.ds(half * NX * CHUNK, NX * CHUNK)
            s = lax.dot_general(k2[rows, :], qb, MATMUL, preferred_element_type=F32)
            parts = []
            for x in range(NX):
                e = jnp.exp2(s[x * CHUNK : (x + 1) * CHUNK])
                keep = kept(e, x * SPAN + half * CHUNK, at)
                parts.append(jnp.where(keep, e, 0.0).astype(BF16))
            weights = jnp.concatenate(parts, axis=0)
            total = total + lax.dot_general(vt[:, rows], weights, MATMUL, preferred_element_type=F32)
        acc[:, cols] = total
        return carry

    lax.fori_loop(zk // 2, COLS // QB, body, 0)


def slow_blocks(zk, q2, qpos, k2, vt, acc, top):
    def body(i, carry):
        b, seg = i // (NC * NX), i % (NC * NX)
        cols = pl.ds(pl.multiple_of(b * QB, QB), QB)
        base = zk * KEYS + (seg % NX) * SPAN + (seg // NX) * CHUNK
        rows = pl.ds(pl.multiple_of(seg * CHUNK, CHUNK), CHUNK)
        s = lax.dot_general(k2[rows, :], q2[:, cols], MATMUL, preferred_element_type=F32)
        keep = kept(s, base, qpos[:, cols])
        s = jnp.where(keep, s, -1e30)
        old = top[:1, cols]
        new = jnp.maximum(old, jnp.max(s, axis=0, keepdims=True))
        weights = jnp.where(keep, jnp.exp2(s - new), 0.0).astype(BF16)
        acc[:, cols] = acc[:, cols] * jnp.exp2(old - new) + lax.dot_general(
            vt[:, rows], weights, MATMUL, preferred_element_type=F32
        )
        top[:, cols] = jnp.broadcast_to(new, (8, QB))
        return carry

    lax.fori_loop(0, COLS // QB * NC * NX, body, 0)


def in_range(q2, kmax):
    most = jnp.broadcast_to(jnp.max(kmax[...], axis=0, keepdims=True), (8, 128)).astype(BF16)
    bound = lax.dot_general(most, jnp.abs(q2[...]), MATMUL, preferred_element_type=F32)
    return jnp.max(bound) <= LIMIT


def write_out(acc, o_ref):
    mixed = acc[:HEAD_DIM, :] / acc[HEAD_DIM : HEAD_DIM + 1, :]
    rows = mixed.T.reshape(NZ * NX, PIECE // 8, 8, HEAD_DIM)
    for g in range(NY):
        o_ref[:, g] = jnp.concatenate([rows[:, g], rows[:, NY + g // 2]], axis=-1).astype(BF16)


def attend_kernel(q2, qpos, kv_ref, kv_all, o_ref, k2, vt, acc, kmax, top, held, sem):
    zk = pl.program_id(0)

    @pl.when(zk == 0)
    def _():
        acc[...] = jnp.zeros_like(acc)
        kmax[...] = jnp.zeros_like(kmax)
        vt[HEAD_DIM:, :] = jnp.ones((VROWS - HEAD_DIM, KEYS), BF16)

    load_keys(kv_ref[...], k2, vt, kmax)
    fast_blocks(zk, q2, qpos, k2, vt, acc)

    @pl.when(zk == NZ - 1)
    def _():
        @pl.when(jnp.logical_not(in_range(q2, kmax)))
        def _():
            acc[...] = jnp.zeros_like(acc)
            top[...] = jnp.full(top.shape, -1e30, F32)

            def block(z, carry):
                copy = pltpu.make_async_copy(kv_all.at[pl.ds(pl.multiple_of(z * KEYS, KEYS), KEYS)], held, sem)
                copy.start()
                copy.wait()
                load_keys(held[...], k2, vt, kmax)
                slow_blocks(z, q2, qpos, k2, vt, acc, top)
                return carry

            lax.fori_loop(0, NZ, block, 0)

        write_out(acc, o_ref)


def attend(q2, qpos, kv_all):
    return pl.pallas_call(
        attend_kernel,
        grid=(NZ,),
        in_specs=[
            pl.BlockSpec((128, COLS), lambda i: (0, 0)),
            pl.BlockSpec((1, COLS), lambda i: (0, 0)),
            pl.BlockSpec((KEYS, 128), lambda i: (i, 0)),
            pl.BlockSpec(memory_space=pl.ANY),
        ],
        out_specs=pl.BlockSpec((NZ * NX, NY, 8, 128), lambda i: (0, 0, 0, 0)),
        out_shape=jax.ShapeDtypeStruct((NZ * NX, NY, 8, 128), BF16),
        scratch_shapes=[
            pltpu.VMEM((KEYS, 128), BF16),
            pltpu.VMEM((VROWS, KEYS), BF16),
            pltpu.VMEM((VROWS, COLS), F32),
            pltpu.VMEM((8, 128), F32),
            pltpu.VMEM((8, COLS), F32),
            pltpu.VMEM((KEYS, 128), BF16),
            pltpu.SemaphoreType.DMA,
        ],
        compiler_params=pltpu.CompilerParams(vmem_limit_bytes=40 << 20, dimension_semantics=("arbitrary",)),
        name="attend",
    )(q2, qpos, kv_all, kv_all)


def project_kernel(parity, r_ref, w_ref, o_ref, rows):
    got = r_ref[...].astype(F32).reshape(NZ, NX, NY, 8, 128)
    left, right = [], []
    lane = lax.broadcasted_iota(jnp.int32, (NZ, 8, 128), 2) < HEAD_DIM
    for y in range(NY):
        for x in range(0, NX, 2):
            a, b = got[:, x, y], got[:, x + 1, y]
            left.append(jnp.where(lane, a, pltpu.roll(b, HEAD_DIM, 2)).reshape(NZ * 8, 128))
            right.append(jnp.where(lane, pltpu.roll(a, HEAD_DIM, 2), b).reshape(NZ * 8, 128))
    w = w_ref[...]
    first = jnp.dot(jnp.concatenate(left, axis=1).astype(BF16), w, preferred_element_type=F32)
    second = jnp.dot(jnp.concatenate(right, axis=1).astype(BF16), w, preferred_element_type=F32)
    odd = parity[0] == 1
    for z in range(NZ):
        rows[12 * z : 12 * z + 8, :] = first[8 * z : 8 * z + 8]
        group = second[8 * z : 8 * z + 8]
        rows[12 * z + 8 : 12 * z + 12, :] = jnp.where(odd, group[4:], group[:4])
    o_ref[...] = rows[...].astype(BF16)


def per_device(queries, key_rows, value_rows, out_weight):
    z, c, y = lax.axis_index("z"), lax.axis_index("c"), lax.axis_index("y")
    vmem = functools.partial(pl.BlockSpec, memory_space=pltpu.VMEM)
    k4 = key_rows.reshape(CHUNK, NX, HEAD_DIM)
    v4 = value_rows.reshape(CHUNK, NX, HEAD_DIM)
    kv = jnp.transpose(jnp.concatenate([k4, v4], axis=2), (1, 0, 2))
    kv = lax.all_to_all(kv, "x", 0, 0, tiled=True).reshape(NX * CHUNK, 128)
    kv_all = lax.all_gather(kv, ("z", "c"), axis=0, tiled=True)
    weight = lax.all_gather(out_weight, "y", axis=0, tiled=True)

    q = queries.reshape(NY, NZ, 12, NX, HEAD_DIM)
    q = jnp.transpose(q, (1, 3, 0, 2, 4))
    q = jnp.concatenate(
        [q[:, :, :, :8].reshape(NZ, NX, 32, HEAD_DIM), q[:, :, :, 8:].reshape(NZ, NX, 16, HEAD_DIM)], axis=2
    )
    q = lax.all_to_all(q.reshape(NZ * NX, PIECE, HEAD_DIM), ("z", "x"), 0, 0, tiled=True)
    q2 = pl.pallas_call(
        prepare_queries, out_shape=jax.ShapeDtypeStruct((128, COLS), BF16), name="prepare_queries"
    )(q.reshape(COLS, HEAD_DIM))
    qpos = (jnp.asarray(query_offsets()) + (CHUNK * c + 12 * z).astype(jnp.int32)).reshape(1, COLS)

    out = attend(q2, qpos, kv_all)
    out = lax.all_to_all(out.reshape(NZ * NX * NY, 8, 128), ("z", "x", "y"), 0, 0, tiled=True)
    return pl.pallas_call(
        project_kernel,
        in_specs=[pl.BlockSpec(memory_space=pltpu.SMEM), vmem(), vmem()],
        out_specs=vmem(),
        out_shape=jax.ShapeDtypeStruct((96, 1024), BF16),
        scratch_shapes=[pltpu.VMEM((96, 1024), F32)],
        compiler_params=pltpu.CompilerParams(vmem_limit_bytes=24 << 20),
        name="project",
    )((y % 2).astype(jnp.int32).reshape(1), out, weight)


def solution(mesh):
    split = Mesh(mesh.devices.reshape(NZ, NX, NC, NY), ("z", "x", "c", "y"))
    rows = ("z", "x", "c")
    return jax.shard_map(
        per_device,
        mesh=split,
        in_specs=(P(rows, "y"), P(rows, "y"), P(rows, "y"), P("y", None)),
        out_specs=P((*rows, "y"), None),
        check_vma=False,
    )
```

```python
import functools
import math

import jax
import jax.numpy as jnp
from jax import lax
from jax.experimental import pallas as pl
from jax.experimental.pallas import tpu as pltpu
from jax.sharding import Mesh, PartitionSpec as P

HEAD_DIM = 64
F32 = jnp.float32
BF16 = jnp.bfloat16
MATMUL = (((1,), (0,)), ((), ()))

NZ, NX, NC, NY = 8, 4, 2, 4
CHUNK = 384
COLS = NX * CHUNK
SPAN = NC * CHUNK
WIDE = COLS // 2
VROWS = 80
LIMIT = 90.0
VMEM_LIMIT = 40 << 20


def whole():
    return pl.BlockSpec(memory_space=pltpu.VMEM)


def scalars():
    return pl.BlockSpec(memory_space=pltpu.SMEM)


def anywhere():
    return pl.BlockSpec(memory_space=pl.ANY)


def split_kernel(place, k_ref, v_ref, q_ref, *outs):
    shift = lax.rem(COLS - HEAD_DIM * place[1], NX * HEAD_DIM)
    k, v, q = (pltpu.roll(r[...].astype(F32), shift, 1) for r in (k_ref, v_ref, q_ref))
    for d in range(NX):
        cols = slice(d * HEAD_DIM, (d + 1) * HEAD_DIM)
        outs[d][...] = jnp.concatenate([k[:, cols], v[:, cols]], axis=1).astype(BF16)
        outs[NX + d][...] = q[:, cols].astype(BF16)


def queries_kernel(*refs):
    for d in range(NX):
        q = refs[d][...].astype(F32) * (math.log2(math.e) / math.sqrt(HEAD_DIM))
        high = q.astype(BF16).astype(F32)
        both = jnp.concatenate([high, q - high], axis=1)
        refs[NX][:, d * CHUNK : (d + 1) * CHUNK] = both.T.astype(BF16)


def load_keys(kv, rows, k2, vt, kmax):
    keys, values = kv[:, :HEAD_DIM], kv[:, HEAD_DIM:]
    twice = jnp.concatenate([keys, keys], axis=1)
    k2[:rows, :] = twice
    vt[:HEAD_DIM, :rows] = values.T
    vt[HEAD_DIM:, :rows] = jnp.ones((VROWS - HEAD_DIM, rows), BF16)
    largest = jnp.max(jnp.abs(twice.astype(F32)).reshape(rows // 8, 8, 128), axis=0)
    kmax[...] = jnp.maximum(kmax[...], largest)


def segment(place, d):
    return lax.rem(place[1] - d + NX, NX)


def all_before(count, rows, needed, q2, k2, vt, acc):
    def body(i, carry):
        block = i // (COLS // WIDE)

        @pl.when(needed[block] == 1)
        def _():
            cols = pl.ds(pl.multiple_of(lax.rem(i, COLS // WIDE) * WIDE, WIDE), WIDE)
            qb = q2[:, cols]
            total = acc[:, cols]
            for start in range(0, rows, WIDE):
                part = slice(start, start + WIDE)
                s = lax.dot_general(k2[block, part, :], qb, MATMUL, preferred_element_type=F32)
                weights = jnp.exp2(s).astype(BF16)
                total = total + lax.dot_general(vt[block, :, part], weights, MATMUL, preferred_element_type=F32)
            acc[:, cols] = total

        return carry

    lax.fori_loop(0, count * (COLS // WIDE), body, 0)


def diagonal(place, parity, q2, k2, vt, acc):
    ahead = lax.broadcasted_iota(jnp.int32, (CHUNK, CHUNK), 0) - lax.broadcasted_iota(jnp.int32, (CHUNK, CHUNK), 1)

    def body(d, carry):
        cols = pl.ds(pl.multiple_of(d * CHUNK, CHUNK), CHUNK)
        s = lax.dot_general(k2[...], q2[:, cols], MATMUL, preferred_element_type=F32)
        parts = []
        for e in range(NX):
            far = SPAN * (segment(place, d) - segment(place, e)) + CHUNK * (place[2] - parity)
            w = jnp.exp2(s[e * CHUNK : (e + 1) * CHUNK])
            parts.append(jnp.where(ahead <= far, w, 0.0).astype(BF16))
        weights = jnp.concatenate(parts, axis=0)
        acc[:, cols] += lax.dot_general(vt[...], weights, MATMUL, preferred_element_type=F32)
        return carry

    lax.fori_loop(0, NX, body, 0)


def step_kernel(rows, place, needed, q2, *refs):
    blocks, (acc_in, kmax_in, acc, kmax, k2, vt) = refs[:-6], refs[-6:]
    acc[...] = acc_in[...]
    kmax[...] = kmax_in[...]
    for i, block in enumerate(blocks):

        @pl.when(needed[i] == 1)
        def _(i=i, block=block):
            load_keys(block[...], rows, k2.at[i], vt.at[i], kmax)

    all_before(len(blocks), rows, needed, q2, k2, vt, acc)


def first_kernel(place, q2, own, other, acc, kmax, k2, vt):
    acc[...] = jnp.zeros_like(acc)
    kmax[...] = jnp.zeros_like(kmax)
    for block, parity in ((own, place[2]), (other, 1 - place[2])):
        load_keys(block[...], COLS, k2.at[0], vt.at[0], kmax)
        diagonal(place, parity, q2, k2.at[0], vt.at[0], acc)


def in_range(q2, kmax):
    most = jnp.broadcast_to(jnp.max(kmax[...], axis=0, keepdims=True), (8, 128)).astype(BF16)
    bound = lax.dot_general(most, jnp.abs(q2[...]), MATMUL, preferred_element_type=F32)
    return jnp.max(bound) <= LIMIT


def slow_block(place, zk, parity, begin, block, q2, acc, top, held, k2, vt, kmax, sem):
    ahead = lax.broadcasted_iota(jnp.int32, (CHUNK, CHUNK), 0) - lax.broadcasted_iota(jnp.int32, (CHUNK, CHUNK), 1)

    def one(e, carry):
        copy = pltpu.make_async_copy(block.at[pl.ds(pl.multiple_of(e * CHUNK, CHUNK), CHUNK)], held, sem)
        copy.start()
        copy.wait()
        load_keys(held[...], CHUNK, k2, vt, kmax)

        def body(d, carry):
            far = (
                NX * SPAN * (place[0] - zk)
                + SPAN * (segment(place, d) - segment(place, e + begin))
                + CHUNK * (place[2] - parity)
            )
            cols = pl.ds(pl.multiple_of(d * CHUNK, CHUNK), CHUNK)
            s = lax.dot_general(k2[:CHUNK, :], q2[:, cols], MATMUL, preferred_element_type=F32)
            keep = ahead <= far
            old = top[:1, cols]
            new = jnp.maximum(old, jnp.max(jnp.where(keep, s, -1e30), axis=0, keepdims=True))
            weights = jnp.where(keep, jnp.exp2(s - new), 0.0).astype(BF16)
            acc[:, cols] = acc[:, cols] * jnp.exp2(old - new) + lax.dot_general(
                vt[:, :CHUNK], weights, MATMUL, preferred_element_type=F32
            )
            top[:, cols] = jnp.broadcast_to(new, (8, CHUNK))
            return carry

        return lax.fori_loop(0, NX, body, carry)

    lax.fori_loop(0, block.shape[0] // CHUNK, one, 0)


def last_kernel(rows, count, entries, place, needed, q2, *refs):
    blocks, kept = refs[:count], refs[count : count + len(entries)]
    acc_in, kmax_in, o_ref, acc, kmax, k2, vt, top, held, sem = refs[count + len(entries) :]
    step_kernel(rows, place, needed, q2, *blocks, acc_in, kmax_in, acc, kmax, k2, vt)

    @pl.when(jnp.logical_not(in_range(q2, kmax)))
    def _():
        acc[...] = jnp.zeros_like(acc)
        top[...] = jnp.full(top.shape, -1e30, F32)
        for block, (step, other, begin) in zip(kept, entries):
            zk = lax.rem(place[0] + step + NZ, NZ)
            parity = 1 - place[2] if other else place[2]

            @pl.when(zk <= place[0])
            def _(block=block, zk=zk, parity=parity, begin=begin):
                slow_block(place, zk, parity, begin, block, q2, acc, top, held, k2.at[0], vt.at[0], kmax, sem)

    mixed = (acc[:HEAD_DIM, :] / acc[HEAD_DIM : HEAD_DIM + 1, :]).T
    for d in range(NX):
        part = mixed[d * CHUNK : (d + 1) * CHUNK].reshape(NY, 2, CHUNK // NY // 2, HEAD_DIM)
        both = jnp.concatenate([part[:, 0], part[:, 1]], axis=-1).astype(BF16)
        o_ref[pl.ds(segment(place, d), 1)] = both.reshape(1, *both.shape)


def project_kernel(place, r_ref, *refs):
    lane = lax.broadcasted_iota(jnp.int32, (CHUNK // NY // 2, 128), 1) < HEAD_DIM
    upper = lower = 0.0
    for d in range(NY):
        y = lax.rem(place[3] - d + NY, NY)
        left, right = [], []
        for x in range(0, NX, 2):
            a = r_ref[pl.ds(x * NY + y, 1)][0].astype(F32)
            b = r_ref[pl.ds((x + 1) * NY + y, 1)][0].astype(F32)
            left.append(jnp.where(lane, a, pltpu.roll(b, HEAD_DIM, 1)))
            right.append(jnp.where(lane, pltpu.roll(a, HEAD_DIM, 1), b))
        w = refs[d][...]
        upper += jnp.dot(jnp.concatenate(left, axis=1).astype(BF16), w, preferred_element_type=F32)
        lower += jnp.dot(jnp.concatenate(right, axis=1).astype(BF16), w, preferred_element_type=F32)
    refs[NY][...] = jnp.concatenate([upper, lower], axis=0).astype(BF16)


STATE = [jax.ShapeDtypeStruct((VROWS, COLS), F32), jax.ShapeDtypeStruct((8, 128), F32)]


def room(count, rows):
    return [pltpu.VMEM((count, rows, 128), BF16), pltpu.VMEM((count, VROWS, rows), BF16)]


def params():
    return pltpu.CompilerParams(vmem_limit_bytes=VMEM_LIMIT)


def cost(keys):
    return pl.CostEstimate(flops=keys, bytes_accessed=keys, transcendentals=0)


def first_step(place, q2, own, other):
    return pl.pallas_call(
        first_kernel,
        in_specs=[scalars(), whole(), whole(), whole()],
        out_specs=[whole(), whole()],
        out_shape=STATE,
        scratch_shapes=room(1, COLS),
        compiler_params=params(),
        cost_estimate=cost(2 * COLS),
        name="own_block",
    )(place, q2, own, other)


def next_step(place, needed, q2, blocks, state, name):
    n = len(blocks)
    rows = blocks[0].shape[0]
    return pl.pallas_call(
        functools.partial(step_kernel, rows),
        in_specs=[scalars(), scalars()] + [whole()] * (n + 3),
        out_specs=[whole(), whole()],
        out_shape=STATE,
        input_output_aliases={n + 3: 0, n + 4: 1},
        scratch_shapes=room(n, rows),
        compiler_params=params(),
        cost_estimate=cost(n * rows),
        name=name,
    )(place, needed, q2, *blocks, *state)


def last_step(place, needed, q2, blocks, state, kept, entries):
    n = len(blocks)
    rows = blocks[0].shape[0]
    return pl.pallas_call(
        functools.partial(last_kernel, rows, n, entries),
        in_specs=[scalars(), scalars()] + [whole()] * (n + 1) + [anywhere()] * len(kept) + [whole()] * 2,
        out_specs=whole(),
        out_shape=jax.ShapeDtypeStruct((NX, NY, CHUNK // NY // 2, 128), BF16),
        scratch_shapes=[
            pltpu.VMEM((VROWS, COLS), F32),
            pltpu.VMEM((8, 128), F32),
            *room(n, rows),
            pltpu.VMEM((8, COLS), F32),
            pltpu.VMEM((CHUNK, 128), BF16),
            pltpu.SemaphoreType.DMA,
        ],
        compiler_params=params(),
        cost_estimate=cost(n * rows),
        name="last_block",
    )(place, needed, q2, *blocks, *kept, *state)


def move(a, axis, size, by):
    return lax.ppermute(a, axis, [(i, (i + by) % size) for i in range(size)])


def per_device(queries, key_rows, value_rows, out_weight):
    z = lax.axis_index("z")
    place = jnp.stack([lax.axis_index(a) for a in ("z", "x", "c", "y")]).astype(jnp.int32)
    pieces = pl.pallas_call(
        split_kernel,
        in_specs=[scalars()] + [whole()] * 3,
        out_specs=[whole()] * (2 * NX),
        out_shape=[jax.ShapeDtypeStruct((CHUNK, 128), BF16)] * NX
        + [jax.ShapeDtypeStruct((CHUNK, HEAD_DIM), BF16)] * NX,
        compiler_params=params(),
        name="split_heads",
    )(place, key_rows, value_rows, queries)
    kv = [pieces[0]] + [move(pieces[d], "x", NX, d) for d in range(1, NX)]
    own = jnp.concatenate(kv, axis=0)
    up = down = own
    other = move(own, "c", NC, 1)
    q = [pieces[NX]] + [move(pieces[NX + d], "x", NX, d) for d in range(1, NX)]
    q2 = pl.pallas_call(
        queries_kernel,
        out_shape=jax.ShapeDtypeStruct((128, COLS), BF16),
        compiler_params=params(),
        name="scale_queries",
    )(*q)
    weights = [out_weight] + [move(out_weight, "y", NY, d) for d in range(1, NY)]
    state = first_step(place, q2, own, other)
    kept, entries = [own, other], [(0, False, 0), (0, True, 0)]
    half = COLS // 2
    for t in range(1, NZ // 2 + 1):
        if t == NZ // 2:
            up, down = up[:half], down[half:]
        up, down = move(up, "z", NZ, 1), move(down, "z", NZ, -1)
        if t == 2:
            up, down, state, weights = lax.optimization_barrier((up, down, state, weights))
        else:
            up, down, state = lax.optimization_barrier((up, down, state))
        other_up, other_down = move(up, "c", NC, 1), move(down, "c", NC, 1)
        needed = jnp.stack([z >= t, z + t >= NZ]).astype(jnp.int32)
        first = 0 if t < NZ // 2 else NX // 2
        kept += [up, down, other_up, other_down]
        entries += [(-t, False, 0), (t, False, first), (-t, True, 0), (t, True, first)]
        if t < NZ // 2:
            state = next_step(place, needed, q2, [up, down], state, "blocks_%d" % t)
            state = next_step(place, needed, q2, [other_up, other_down], state, "other_blocks_%d" % t)
        else:
            needed = jnp.concatenate([needed, needed])
            out = last_step(place, needed, q2, [up, down, other_up, other_down], state, kept, tuple(entries))

    out = lax.all_to_all(out.reshape(NX * NY, CHUNK // NY // 2, 128), ("x", "y"), 0, 0, tiled=True)
    return pl.pallas_call(
        project_kernel,
        in_specs=[scalars()] + [whole()] * (1 + NY),
        out_specs=whole(),
        out_shape=jax.ShapeDtypeStruct((CHUNK // NY, 1024), BF16),
        compiler_params=params(),
        name="project",
    )(place, out, *weights)


def solution(mesh):
    split = Mesh(mesh.devices.reshape(NZ, NX, NC, NY), ("z", "x", "c", "y"))
    rows = ("z", "x", "c")
    return jax.shard_map(
        per_device,
        mesh=split,
        in_specs=(P(rows, "y"), P(rows, "y"), P(rows, "y"), P("y", None)),
        out_specs=P((*rows, "y"), None),
        check_vma=False,
    )
```

```python
import functools
import math

import jax
import jax.numpy as jnp
from jax import lax
from jax.experimental import pallas as pl
from jax.experimental.pallas import tpu as pltpu
from jax.sharding import Mesh, PartitionSpec as P

HEAD_DIM = 64
F32 = jnp.float32
BF16 = jnp.bfloat16
MATMUL = (((1,), (0,)), ((), ()))

NZ, NX, NC, NY = 8, 4, 2, 4
CHUNK = 384
COLS = NX * CHUNK
SPAN = NC * CHUNK
WIDE = COLS // 2
VROWS = 80
LIMIT = 90.0
VMEM_LIMIT = 40 << 20


def whole():
    return pl.BlockSpec(memory_space=pltpu.VMEM)


def scalars():
    return pl.BlockSpec(memory_space=pltpu.SMEM)


def anywhere():
    return pl.BlockSpec(memory_space=pl.ANY)


def in_hbm():
    return pl.BlockSpec(memory_space=pltpu.HBM)


def split_kernel(place, k_hbm, v_hbm, q_hbm, *refs):
    outs, (k_ref, v_ref, q_ref, sems) = refs[: 2 * NX], refs[2 * NX :]
    pairs = ((k_hbm, k_ref), (v_hbm, v_ref), (q_hbm, q_ref))
    copies = [pltpu.make_async_copy(src, dst, sems.at[i]) for i, (src, dst) in enumerate(pairs)]
    for copy in copies:
        copy.start()
    for copy in copies:
        copy.wait()
    shift = lax.rem(COLS - HEAD_DIM * place[1], NX * HEAD_DIM)
    k, v, q = (pltpu.roll(r[...].astype(F32), shift, 1) for r in (k_ref, v_ref, q_ref))
    for d in range(NX):
        cols = slice(d * HEAD_DIM, (d + 1) * HEAD_DIM)
        outs[d][...] = jnp.concatenate([k[:, cols], v[:, cols]], axis=1).astype(BF16)
        outs[NX + d][...] = q[:, cols].astype(BF16)


def queries_kernel(*refs):
    for d in range(NX):
        q = refs[d][...].astype(F32) * (math.log2(math.e) / math.sqrt(HEAD_DIM))
        high = q.astype(BF16).astype(F32)
        both = jnp.concatenate([high, q - high], axis=1)
        refs[NX][:, d * CHUNK : (d + 1) * CHUNK] = both.T.astype(BF16)


def load_keys(kv, rows, k2, vt, kmax):
    keys, values = kv[:, :HEAD_DIM], kv[:, HEAD_DIM:]
    twice = jnp.concatenate([keys, keys], axis=1)
    k2[:rows, :] = twice
    vt[:HEAD_DIM, :rows] = values.T
    vt[HEAD_DIM:, :rows] = jnp.ones((VROWS - HEAD_DIM, rows), BF16)
    largest = jnp.max(jnp.abs(twice.astype(F32)).reshape(rows // 8, 8, 128), axis=0)
    kmax[...] = jnp.maximum(kmax[...], largest)


def segment(place, d):
    return lax.rem(place[1] - d + NX, NX)


def owner(place, half):
    return place[0] if half == 0 else NZ - 1 - place[0]


def source(place, step, other):
    ahead = (place[2] == 1) != other
    return lax.rem(place[0] + jnp.where(ahead, step, NZ - step), NZ)


def all_before(rows, half, q2, k2, vt, acc):
    cols = slice(half * WIDE, (half + 1) * WIDE)

    def body(i, carry):
        qb = q2[:, cols]
        total = acc[:, cols]
        for j in range(2):
            part = pl.ds(pl.multiple_of((2 * i + j) * WIDE, WIDE), WIDE)
            s = lax.dot_general(k2[part, :], qb, MATMUL, preferred_element_type=F32)
            weights = jnp.exp2(s).astype(BF16)
            total = total + lax.dot_general(vt[:, part], weights, MATMUL, preferred_element_type=F32)
        acc[:, cols] = total
        return carry

    lax.fori_loop(0, rows // WIDE // 2, body, 0)


def diagonal(place, half, first, q2, k2, vt, acc):
    ahead = lax.broadcasted_iota(jnp.int32, (CHUNK, CHUNK), 0) - lax.broadcasted_iota(jnp.int32, (CHUNK, CHUNK), 1)

    def body(i, carry):
        d = NX // 2 * half + lax.rem(i, NX // 2)
        parity = jnp.where(i < NX // 2, first, 1 - first)
        cols = pl.ds(pl.multiple_of(d * CHUNK, CHUNK), CHUNK)
        rows = pl.multiple_of((i // (NX // 2)) * COLS, COLS)
        s = lax.dot_general(k2[pl.ds(rows, COLS), :], q2[:, cols], MATMUL, preferred_element_type=F32)
        parts = []
        for e in range(NX):
            far = SPAN * (segment(place, d) - segment(place, e)) + CHUNK * (place[2] - parity)
            w = jnp.exp2(s[e * CHUNK : (e + 1) * CHUNK])
            parts.append(jnp.where(ahead <= far, w, 0.0).astype(BF16))
        weights = jnp.concatenate(parts, axis=0)
        acc[:, cols] += lax.dot_general(vt[:, pl.ds(rows, COLS)], weights, MATMUL, preferred_element_type=F32)
        return carry

    lax.fori_loop(0, NX, body, 0)


def add_block(step, other, place, block, q2, acc, kmax, k2, vt):
    zk = source(place, step, other)
    rows = block.shape[0]

    @pl.when(jnp.logical_or(zk <= owner(place, 0), zk <= owner(place, 1)))
    def _():
        load_keys(block[...], rows, k2, vt, kmax)

    for half in range(2):

        @pl.when(zk < owner(place, half))
        def _(half=half):
            all_before(rows, half, q2, k2, vt, acc)

        if (step == 0 and half == 0) or (step % 2 == 1 and half == 1):

            @pl.when(zk == owner(place, half))
            def _(half=half):
                first = 1 - place[2] if other else place[2]
                diagonal(place, half, first, q2, k2, vt, acc)


def step_kernel(step, other, place, q2, block, acc_in, kmax_in, acc, kmax, k2, vt):
    acc[...] = acc_in[...]
    kmax[...] = kmax_in[...]
    add_block(step, other, place, block, q2, acc, kmax, k2, vt)


def first_kernel(place, q2, block, acc, kmax, k2, vt):
    acc[...] = jnp.zeros_like(acc)
    kmax[...] = jnp.zeros_like(kmax)
    add_block(0, False, place, block, q2, acc, kmax, k2, vt)


def in_range(q2, kmax):
    most = jnp.broadcast_to(jnp.max(kmax[...], axis=0, keepdims=True), (8, 128)).astype(BF16)
    bound = lax.dot_general(most, jnp.abs(q2[...]), MATMUL, preferred_element_type=F32)
    return jnp.max(bound) <= LIMIT


def slow_block(place, zk, first, block, q2, acc, top, held, k2, vt, kmax, sem):
    ahead = lax.broadcasted_iota(jnp.int32, (CHUNK, CHUNK), 0) - lax.broadcasted_iota(jnp.int32, (CHUNK, CHUNK), 1)

    def one(e, carry):
        copy = pltpu.make_async_copy(block.at[pl.ds(pl.multiple_of(e * CHUNK, CHUNK), CHUNK)], held, sem)
        copy.start()
        copy.wait()
        load_keys(held[...], CHUNK, k2, vt, kmax)
        parity = jnp.where(e < NX, first, 1 - first)

        def body(d, carry):
            far = (
                NX * SPAN * (jnp.where(d < NX // 2, owner(place, 0), owner(place, 1)) - zk)
                + SPAN * (segment(place, d) - segment(place, lax.rem(e, NX)))
                + CHUNK * (place[2] - parity)
            )
            cols = pl.ds(pl.multiple_of(d * CHUNK, CHUNK), CHUNK)
            s = lax.dot_general(k2[:CHUNK, :], q2[:, cols], MATMUL, preferred_element_type=F32)
            keep = ahead <= far
            old = top[:1, cols]
            new = jnp.maximum(old, jnp.max(jnp.where(keep, s, -1e30), axis=0, keepdims=True))
            weights = jnp.where(keep, jnp.exp2(s - new), 0.0).astype(BF16)
            acc[:, cols] = acc[:, cols] * jnp.exp2(old - new) + lax.dot_general(
                vt[:, :CHUNK], weights, MATMUL, preferred_element_type=F32
            )
            top[:, cols] = jnp.broadcast_to(new, (8, CHUNK))
            return carry

        return lax.fori_loop(0, NX, body, carry)

    lax.fori_loop(0, block.shape[0] // CHUNK, one, 0)


def last_kernel(entries, place, q2, *refs):
    count = len(entries)
    blocks, kept = refs[:2], refs[2 : 2 + count]
    acc_in, kmax_in, *outs = refs[2 + count : 4 + count + NX]
    acc, kmax, k2, vt, top, held, sem = refs[4 + count + NX :]
    acc[...] = acc_in[...]
    kmax[...] = kmax_in[...]
    for block, (step, other) in zip(blocks, entries[-2:]):
        add_block(step, other, place, block, q2, acc, kmax, k2, vt)

    @pl.when(jnp.logical_not(in_range(q2, kmax)))
    def _():
        acc[...] = jnp.zeros_like(acc)
        top[...] = jnp.full(top.shape, -1e30, F32)
        for block, (step, other) in zip(kept, entries):
            first = 1 - place[2] if other else place[2]
            slow_block(place, source(place, step, other), first, block, q2, acc, top, held, k2, vt, kmax, sem)

    mixed = (acc[:HEAD_DIM, :] / acc[HEAD_DIM : HEAD_DIM + 1, :]).T
    for d in range(NX):
        part = mixed[d * CHUNK : (d + 1) * CHUNK].reshape(NY, 2, CHUNK // NY // 2, HEAD_DIM)
        both = jnp.concatenate([part[:, 0], part[:, 1]], axis=-1).astype(BF16)
        for y in range(NY):
            outs[d][pl.ds(lax.rem(y - place[3] + NY, NY), 1)] = both[y : y + 1]


def project_kernel(place, *refs):
    lane = lax.broadcasted_iota(jnp.int32, (CHUNK // NY // 2, 128), 1) < HEAD_DIM
    upper = lower = 0.0
    for e in range(NY):
        left, right = [], []
        for x in range(0, NX, 2):
            a = refs[e][pl.ds(lax.rem(x - place[1] + NX, NX), 1)][0].astype(F32)
            b = refs[e][pl.ds(lax.rem(x + 1 - place[1] + NX, NX), 1)][0].astype(F32)
            left.append(jnp.where(lane, a, pltpu.roll(b, HEAD_DIM, 1)))
            right.append(jnp.where(lane, pltpu.roll(a, HEAD_DIM, 1), b))
        w = refs[NY + e][...]
        upper += jnp.dot(jnp.concatenate(left, axis=1).astype(BF16), w, preferred_element_type=F32)
        lower += jnp.dot(jnp.concatenate(right, axis=1).astype(BF16), w, preferred_element_type=F32)
    refs[2 * NY][...] = jnp.concatenate([upper, lower], axis=0).astype(BF16)


STATE = [jax.ShapeDtypeStruct((VROWS, COLS), F32), jax.ShapeDtypeStruct((8, 128), F32)]


def room(rows):
    return [pltpu.VMEM((rows, 128), BF16), pltpu.VMEM((VROWS, rows), BF16)]


def params():
    return pltpu.CompilerParams(vmem_limit_bytes=VMEM_LIMIT)


def cost(keys):
    return pl.CostEstimate(flops=keys, bytes_accessed=keys, transcendentals=0)


def split_heads(place, key_rows, value_rows, queries):
    return pl.pallas_call(
        split_kernel,
        in_specs=[scalars()] + [in_hbm()] * 3,
        out_specs=[whole()] * (2 * NX),
        out_shape=[jax.ShapeDtypeStruct((CHUNK, 128), BF16)] * NX
        + [jax.ShapeDtypeStruct((CHUNK, HEAD_DIM), BF16)] * NX,
        scratch_shapes=[pltpu.VMEM((CHUNK, NX * HEAD_DIM), BF16)] * 3 + [pltpu.SemaphoreType.DMA((3,))],
        compiler_params=params(),
        name="split_heads",
    )(place, key_rows, value_rows, queries)


def scale_queries(q):
    return pl.pallas_call(
        queries_kernel,
        out_shape=jax.ShapeDtypeStruct((128, COLS), BF16),
        compiler_params=params(),
        name="scale_queries",
    )(*q)


def first_step(place, q2, block):
    return pl.pallas_call(
        first_kernel,
        in_specs=[scalars(), whole(), whole()],
        out_specs=[whole(), whole()],
        out_shape=STATE,
        scratch_shapes=room(block.shape[0]),
        compiler_params=params(),
        cost_estimate=cost(COLS),
        name="own_block",
    )(place, q2, block)


def next_step(place, q2, block, state, step, other):
    return pl.pallas_call(
        functools.partial(step_kernel, step, other),
        in_specs=[scalars()] + [whole()] * 4,
        out_specs=[whole(), whole()],
        out_shape=STATE,
        input_output_aliases={3: 0, 4: 1},
        scratch_shapes=room(block.shape[0]),
        compiler_params=params(),
        cost_estimate=cost(COLS),
        name="block_%d_%d" % (step, other),
    )(place, q2, block, *state)


def last_step(place, q2, blocks, state, kept, entries):
    return pl.pallas_call(
        functools.partial(last_kernel, entries),
        in_specs=[scalars()] + [whole()] * 3 + [anywhere()] * len(kept) + [whole()] * 2,
        out_specs=[whole()] * NX,
        out_shape=[jax.ShapeDtypeStruct((NY, CHUNK // NY // 2, 128), BF16)] * NX,
        scratch_shapes=[
            pltpu.VMEM((VROWS, COLS), F32),
            pltpu.VMEM((8, 128), F32),
            *room(blocks[0].shape[0]),
            pltpu.VMEM((8, COLS), F32),
            pltpu.VMEM((CHUNK, 128), BF16),
            pltpu.SemaphoreType.DMA,
        ],
        compiler_params=params(),
        cost_estimate=cost(COLS),
        name="last_block",
    )(place, q2, *blocks, *kept, *state)


def move(a, axis, size, by):
    return lax.ppermute(a, axis, [(i, (i + by) % size) for i in range(size)])


def move_ring(a):
    pairs = [(z * NC + c, (z + 1 - 2 * c) % NZ * NC + c) for z in range(NZ) for c in range(NC)]
    return lax.ppermute(a, ("z", "c"), pairs)


def move_segment(a, d, back):
    by = -d if back else d
    if d < NX // 2:
        return move(a, "x", NX, by)
    pairs = [(z * NX + x, (NZ - 1 - z) * NX + (x + by) % NX) for z in range(NZ) for x in range(NX)]
    return lax.ppermute(a, ("z", "x"), pairs)


def per_device(queries, key_rows, value_rows, out_weight):
    place = jnp.stack([lax.axis_index(a) for a in ("z", "x", "c", "y")]).astype(jnp.int32)
    pieces = split_heads(place, key_rows, value_rows, queries)
    own = jnp.concatenate([pieces[0]] + [move(pieces[d], "x", NX, d) for d in range(1, NX)], axis=0)
    block = jnp.concatenate([own, move(own, "c", NC, 1)], axis=0)
    q2 = scale_queries([pieces[NX]] + [move_segment(pieces[NX + d], d, False) for d in range(1, NX)])
    weights = [out_weight] + [move(out_weight, "y", NY, e) for e in range(1, NY)]
    state = first_step(place, q2, block)
    kept, entries = [block], [(0, False)]
    for t in range(1, NZ // 2 + 1):
        if t == NZ // 2:
            block = block[:COLS]
        block = move_ring(block)
        if t == 3:
            block, state, weights = lax.optimization_barrier((block, state, weights))
        else:
            block, state = lax.optimization_barrier((block, state))
        other = move(block, "c", NC, 1)
        kept += [block, other]
        entries += [(t, False), (t, True)]
        if t < NZ // 2:
            state = next_step(place, q2, block, state, t, False)
            state = next_step(place, q2, other, state, t, True)
    out = last_step(place, q2, [block, other], state, kept, tuple(entries))
    out = [out[0]] + [move_segment(out[d], d, True) for d in range(1, NX)]
    out = [jnp.stack([out[d][e] for d in range(NX)]) for e in range(NY)]
    out = [out[0]] + [move(out[e], "y", NY, e) for e in range(1, NY)]
    return pl.pallas_call(
        project_kernel,
        in_specs=[scalars()] + [whole()] * (2 * NY),
        out_specs=whole(),
        out_shape=jax.ShapeDtypeStruct((CHUNK // NY, 1024), BF16),
        compiler_params=params(),
        name="project",
    )(place, *out, *weights)


def solution(mesh):
    split = Mesh(mesh.devices.reshape(NZ, NX, NC, NY), ("z", "x", "c", "y"))
    rows = ("z", "x", "c")
    return jax.shard_map(
        per_device,
        mesh=split,
        in_specs=(P(rows, "y"), P(rows, "y"), P(rows, "y"), P("y", None)),
        out_specs=P((*rows, "y"), None),
        check_vma=False,
    )
```

```python
import functools
import math

import jax
import jax.numpy as jnp
from jax import lax
from jax.experimental import pallas as pl
from jax.experimental.pallas import tpu as pltpu
from jax.sharding import Mesh, PartitionSpec as P

HEAD_DIM = 64
F32 = jnp.float32
BF16 = jnp.bfloat16
MATMUL = (((1,), (0,)), ((), ()))

NZ, NX, NC, NY = 8, 4, 2, 4
CHUNK = 384
COLS = NX * CHUNK
SPAN = NC * CHUNK
WIDE = COLS // 2
VROWS = 80
LIMIT = 90.0
VMEM_LIMIT = 40 << 20


def whole():
    return pl.BlockSpec(memory_space=pltpu.VMEM)


def scalars():
    return pl.BlockSpec(memory_space=pltpu.SMEM)


def anywhere():
    return pl.BlockSpec(memory_space=pl.ANY)


def in_hbm():
    return pl.BlockSpec(memory_space=pltpu.HBM)


def split_kernel(place, k_hbm, v_hbm, q_hbm, *refs):
    outs, (k_ref, v_ref, q_ref, sems) = refs[: 2 * NX], refs[2 * NX :]
    pairs = ((k_hbm, k_ref), (v_hbm, v_ref), (q_hbm, q_ref))
    copies = [pltpu.make_async_copy(src, dst, sems.at[i]) for i, (src, dst) in enumerate(pairs)]
    for copy in copies:
        copy.start()
    for copy in copies:
        copy.wait()
    shift = lax.rem(COLS - HEAD_DIM * place[1], NX * HEAD_DIM)
    k, v, q = (pltpu.roll(r[...].astype(F32), shift, 1) for r in (k_ref, v_ref, q_ref))
    for d in range(NX):
        cols = slice(d * HEAD_DIM, (d + 1) * HEAD_DIM)
        outs[d][...] = jnp.concatenate([k[:, cols], v[:, cols]], axis=1).astype(BF16)
        rows = q[:, cols]
        outs[NX + d][...] = jnp.concatenate([rows[: CHUNK // 2], rows[CHUNK // 2 :]], axis=1).astype(BF16)


def queries_kernel(*refs):
    for d in range(NX):
        q = refs[d][...].astype(F32)
        q = jnp.concatenate([q[:, :HEAD_DIM], q[:, HEAD_DIM:]], axis=0) * (math.log2(math.e) / math.sqrt(HEAD_DIM))
        high = q.astype(BF16).astype(F32)
        both = jnp.concatenate([high, q - high], axis=1)
        refs[NX][:, d * CHUNK : (d + 1) * CHUNK] = both.T.astype(BF16)


def load_keys(kv, rows, k2, vt, kmax):
    keys, values = kv[:, :HEAD_DIM], kv[:, HEAD_DIM:]
    twice = jnp.concatenate([keys, keys], axis=1)
    k2[:rows, :] = twice
    vt[:HEAD_DIM, :rows] = values.T
    vt[HEAD_DIM:, :rows] = jnp.ones((VROWS - HEAD_DIM, rows), BF16)
    largest = jnp.max(jnp.abs(twice.astype(F32)).reshape(rows // 8, 8, 128), axis=0)
    kmax[...] = jnp.maximum(kmax[...], largest)


def segment(place, d):
    return lax.rem(place[1] - d + NX, NX)


def owner(place, half):
    return place[0] if half == 0 else NZ - 1 - place[0]


def source(place, step, other):
    ahead = (place[2] == 1) != other
    return lax.rem(place[0] + jnp.where(ahead, step, NZ - step), NZ)


def all_before(rows, half, q2, k2, vt, acc):
    cols = slice(half * WIDE, (half + 1) * WIDE)

    def body(i, carry):
        qb = q2[:, cols]
        total = acc[:, cols]
        for j in range(2):
            part = pl.ds(pl.multiple_of((2 * i + j) * WIDE, WIDE), WIDE)
            s = lax.dot_general(k2[part, :], qb, MATMUL, preferred_element_type=F32)
            weights = jnp.exp2(s).astype(BF16)
            total = total + lax.dot_general(vt[:, part], weights, MATMUL, preferred_element_type=F32)
        acc[:, cols] = total
        return carry

    lax.fori_loop(0, rows // WIDE // 2, body, 0)


def diagonal(place, half, first, q2, k2, vt, acc):
    ahead = lax.broadcasted_iota(jnp.int32, (CHUNK, CHUNK), 0) - lax.broadcasted_iota(jnp.int32, (CHUNK, CHUNK), 1)

    def body(i, carry):
        d = NX // 2 * half + lax.rem(i, NX // 2)
        parity = jnp.where(i < NX // 2, first, 1 - first)
        cols = pl.ds(pl.multiple_of(d * CHUNK, CHUNK), CHUNK)
        rows = pl.multiple_of((i // (NX // 2)) * COLS, COLS)
        s = lax.dot_general(k2[pl.ds(rows, COLS), :], q2[:, cols], MATMUL, preferred_element_type=F32)
        parts = []
        for e in range(NX):
            far = SPAN * (segment(place, d) - segment(place, e)) + CHUNK * (place[2] - parity)
            w = jnp.exp2(s[e * CHUNK : (e + 1) * CHUNK])
            parts.append(jnp.where(ahead <= far, w, 0.0).astype(BF16))
        weights = jnp.concatenate(parts, axis=0)
        acc[:, cols] += lax.dot_general(vt[:, pl.ds(rows, COLS)], weights, MATMUL, preferred_element_type=F32)
        return carry

    lax.fori_loop(0, NX, body, 0)


def add_block(step, other, place, block, q2, acc, kmax, k2, vt):
    zk = source(place, step, other)
    rows = block.shape[0]

    @pl.when(jnp.logical_or(zk <= owner(place, 0), zk <= owner(place, 1)))
    def _():
        load_keys(block[...], rows, k2, vt, kmax)

    for half in range(2):

        @pl.when(zk < owner(place, half))
        def _(half=half):
            all_before(rows, half, q2, k2, vt, acc)

        if (step == 0 and half == 0) or (step % 2 == 1 and half == 1):

            @pl.when(zk == owner(place, half))
            def _(half=half):
                first = 1 - place[2] if other else place[2]
                diagonal(place, half, first, q2, k2, vt, acc)


def step_kernel(step, other, place, q2, block, acc_in, kmax_in, acc, kmax, k2, vt):
    acc[...] = acc_in[...]
    kmax[...] = kmax_in[...]
    add_block(step, other, place, block, q2, acc, kmax, k2, vt)


def first_kernel(place, q2, block, acc, kmax, k2, vt):
    acc[...] = jnp.zeros_like(acc)
    kmax[...] = jnp.zeros_like(kmax)
    add_block(0, False, place, block, q2, acc, kmax, k2, vt)


def in_range(q2, kmax):
    most = jnp.broadcast_to(jnp.max(kmax[...], axis=0, keepdims=True), (8, 128)).astype(BF16)
    bound = lax.dot_general(most, jnp.abs(q2[...]), MATMUL, preferred_element_type=F32)
    return jnp.max(bound) <= LIMIT


def slow_block(place, zk, first, block, q2, acc, top, held, k2, vt, kmax, sem):
    ahead = lax.broadcasted_iota(jnp.int32, (CHUNK, CHUNK), 0) - lax.broadcasted_iota(jnp.int32, (CHUNK, CHUNK), 1)

    def one(e, carry):
        copy = pltpu.make_async_copy(block.at[pl.ds(pl.multiple_of(e * CHUNK, CHUNK), CHUNK)], held, sem)
        copy.start()
        copy.wait()
        load_keys(held[...], CHUNK, k2, vt, kmax)
        parity = jnp.where(e < NX, first, 1 - first)

        def body(d, carry):
            far = (
                NX * SPAN * (jnp.where(d < NX // 2, owner(place, 0), owner(place, 1)) - zk)
                + SPAN * (segment(place, d) - segment(place, lax.rem(e, NX)))
                + CHUNK * (place[2] - parity)
            )
            cols = pl.ds(pl.multiple_of(d * CHUNK, CHUNK), CHUNK)
            s = lax.dot_general(k2[:CHUNK, :], q2[:, cols], MATMUL, preferred_element_type=F32)
            keep = ahead <= far
            old = top[:1, cols]
            new = jnp.maximum(old, jnp.max(jnp.where(keep, s, -1e30), axis=0, keepdims=True))
            weights = jnp.where(keep, jnp.exp2(s - new), 0.0).astype(BF16)
            acc[:, cols] = acc[:, cols] * jnp.exp2(old - new) + lax.dot_general(
                vt[:, :CHUNK], weights, MATMUL, preferred_element_type=F32
            )
            top[:, cols] = jnp.broadcast_to(new, (8, CHUNK))
            return carry

        return lax.fori_loop(0, NX, body, carry)

    lax.fori_loop(0, block.shape[0] // CHUNK, one, 0)


def last_kernel(entries, place, q2, *refs):
    count = len(entries)
    blocks, kept = refs[:2], refs[2 : 2 + count]
    acc_in, kmax_in, *outs = refs[2 + count : 4 + count + NX]
    acc, kmax, k2, vt, top, held, sem = refs[4 + count + NX :]
    acc[...] = acc_in[...]
    kmax[...] = kmax_in[...]
    for block, (step, other) in zip(blocks, entries[-2:]):
        add_block(step, other, place, block, q2, acc, kmax, k2, vt)

    @pl.when(jnp.logical_not(in_range(q2, kmax)))
    def _():
        acc[...] = jnp.zeros_like(acc)
        top[...] = jnp.full(top.shape, -1e30, F32)
        for block, (step, other) in zip(kept, entries):
            first = 1 - place[2] if other else place[2]
            slow_block(place, source(place, step, other), first, block, q2, acc, top, held, k2, vt, kmax, sem)

    mixed = (acc[:HEAD_DIM, :] / acc[HEAD_DIM : HEAD_DIM + 1, :]).T
    for d in range(NX):
        part = mixed[d * CHUNK : (d + 1) * CHUNK].reshape(NY, 2, CHUNK // NY // 2, HEAD_DIM)
        both = jnp.concatenate([part[:, 0], part[:, 1]], axis=-1).astype(BF16)
        for y in range(NY):
            outs[d][pl.ds(lax.rem(y - place[3] + NY, NY), 1)] = both[y : y + 1]


def project_kernel(place, *refs):
    own, near, far, o_ref = refs[NY:]
    lane = lax.broadcasted_iota(jnp.int32, (CHUNK // NY // 2, 128), 1) < HEAD_DIM
    even = place[2] == 0
    upper = lower = 0.0
    for e in range(NY):
        left, right = [], []
        for x in range(0, NX, 2):
            a = refs[e][pl.ds(lax.rem(x - place[1] + NX, NX), 1)][0].astype(F32)
            b = refs[e][pl.ds(lax.rem(x + 1 - place[1] + NX, NX), 1)][0].astype(F32)
            left.append(jnp.where(lane, a, pltpu.roll(b, HEAD_DIM, 1)))
            right.append(jnp.where(lane, pltpu.roll(a, HEAD_DIM, 1), b))
        if e == 0:
            w = own[...]
        else:
            left, right = ([jnp.where(even, *p), jnp.where(even, *p[::-1])] for p in (left, right))
            w = jnp.concatenate([near[(e - 1) * 128 : e * 128], far[(e - 1) * 128 : e * 128]], axis=0)
        upper += jnp.dot(jnp.concatenate(left, axis=1).astype(BF16), w, preferred_element_type=F32)
        lower += jnp.dot(jnp.concatenate(right, axis=1).astype(BF16), w, preferred_element_type=F32)
    o_ref[...] = jnp.concatenate([upper, lower], axis=0).astype(BF16)


STATE = [jax.ShapeDtypeStruct((VROWS, COLS), F32), jax.ShapeDtypeStruct((8, 128), F32)]


def room(rows):
    return [pltpu.VMEM((rows, 128), BF16), pltpu.VMEM((VROWS, rows), BF16)]


def params():
    return pltpu.CompilerParams(vmem_limit_bytes=VMEM_LIMIT)


def cost(keys):
    return pl.CostEstimate(flops=keys, bytes_accessed=keys, transcendentals=0)


def split_heads(place, key_rows, value_rows, queries):
    return pl.pallas_call(
        split_kernel,
        in_specs=[scalars()] + [in_hbm()] * 3,
        out_specs=[whole()] * (2 * NX),
        out_shape=[jax.ShapeDtypeStruct((CHUNK, 128), BF16)] * NX
        + [jax.ShapeDtypeStruct((CHUNK // 2, 128), BF16)] * NX,
        scratch_shapes=[pltpu.VMEM((CHUNK, NX * HEAD_DIM), BF16)] * 3 + [pltpu.SemaphoreType.DMA((3,))],
        compiler_params=pltpu.CompilerParams(vmem_limit_bytes=60 << 20),
        name="split_heads",
    )(place, key_rows, value_rows, queries)


def scale_queries(q):
    return pl.pallas_call(
        queries_kernel,
        out_shape=jax.ShapeDtypeStruct((128, COLS), BF16),
        compiler_params=params(),
        name="scale_queries",
    )(*q)


def first_step(place, q2, block):
    return pl.pallas_call(
        first_kernel,
        in_specs=[scalars(), whole(), whole()],
        out_specs=[whole(), whole()],
        out_shape=STATE,
        scratch_shapes=room(block.shape[0]),
        compiler_params=params(),
        cost_estimate=cost(COLS),
        name="own_block",
    )(place, q2, block)


def next_step(place, q2, block, state, step, other):
    return pl.pallas_call(
        functools.partial(step_kernel, step, other),
        in_specs=[scalars()] + [whole()] * 4,
        out_specs=[whole(), whole()],
        out_shape=STATE,
        input_output_aliases={3: 0, 4: 1},
        scratch_shapes=room(block.shape[0]),
        compiler_params=params(),
        cost_estimate=cost(COLS),
        name="block_%d_%d" % (step, other),
    )(place, q2, block, *state)


def last_step(place, q2, blocks, state, kept, entries):
    return pl.pallas_call(
        functools.partial(last_kernel, entries),
        in_specs=[scalars()] + [whole()] * 3 + [anywhere()] * len(kept) + [whole()] * 2,
        out_specs=[whole()] * NX,
        out_shape=[jax.ShapeDtypeStruct((NY, CHUNK // NY // 2, 128), BF16)] * NX,
        scratch_shapes=[
            pltpu.VMEM((VROWS, COLS), F32),
            pltpu.VMEM((8, 128), F32),
            *room(blocks[0].shape[0]),
            pltpu.VMEM((8, COLS), F32),
            pltpu.VMEM((CHUNK, 128), BF16),
            pltpu.SemaphoreType.DMA,
        ],
        compiler_params=params(),
        cost_estimate=cost(COLS),
        name="last_block",
    )(place, q2, *blocks, *kept, *state)


def move(a, axis, size, by):
    return lax.ppermute(a, axis, [(i, (i + by) % size) for i in range(size)])


def move_ring(a):
    pairs = [(z * NC + c, (z + 1 - 2 * c) % NZ * NC + c) for z in range(NZ) for c in range(NC)]
    return lax.ppermute(a, ("z", "c"), pairs)


def move_segment(a, d, back):
    by = -d if back else d
    if d < NX // 2:
        return move(a, "x", NX, by)
    pairs = [(z * NX + x, (NZ - 1 - z) * NX + (x + by) % NX) for z in range(NZ) for x in range(NX)]
    return lax.ppermute(a, ("z", "x"), pairs)


def per_device(queries, key_rows, value_rows, out_weight):
    place = jnp.stack([lax.axis_index(a) for a in ("z", "x", "c", "y")]).astype(jnp.int32)
    pieces = split_heads(place, key_rows, value_rows, queries)
    own = jnp.concatenate([pieces[0]] + [move(pieces[d], "x", NX, d) for d in range(1, NX)], axis=0)
    q = [pieces[NX]] + [move_segment(pieces[NX + d], d, False) for d in range(1, NX)]
    half = out_weight.shape[0] // NC
    quarter = half // 2
    mine = lax.dynamic_slice_in_dim(out_weight, place[2] * half, half, 0)
    after, before = move(mine, "y", NY, 1), move(mine, "y", NY, -1)
    block = jnp.concatenate([own, move(own, "c", NC, 1)], axis=0)
    block, q, after, before = lax.optimization_barrier((block, q, after, before))
    q2 = scale_queries(q)
    across = [move(after[:quarter], "y", NY, 1), move(before[quarter:], "y", NY, -1)]
    state = first_step(place, q2, block)
    kept, entries = [block], [(0, False)]
    for t in range(1, NZ // 2 + 1):
        if t == NZ // 2:
            block = block[:COLS]
        block = move_ring(block)
        if t == 1:
            block, state, across = lax.optimization_barrier((block, state, across))
            near = jnp.concatenate([after, *across, before], axis=0)
            far = move(near, "c", NC, 1)
        elif t == 2:
            block, state, near, far = lax.optimization_barrier((block, state, near, far))
        else:
            block, state = lax.optimization_barrier((block, state))
        other = move(block, "c", NC, 1)
        kept += [block, other]
        entries += [(t, False), (t, True)]
        if t < NZ // 2:
            state = next_step(place, q2, block, state, t, False)
            state = next_step(place, q2, other, state, t, True)
    out = last_step(place, q2, [block, other], state, kept, tuple(entries))
    out = [out[0]] + [move_segment(out[d], d, True) for d in range(1, NX)]
    out = [jnp.stack([out[d][e] for d in range(NX)]) for e in range(NY)]
    out = [out[0]] + [move(out[e], "y", NY, e) for e in range(1, NY)]
    return pl.pallas_call(
        project_kernel,
        in_specs=[scalars()] + [whole()] * (NY + 3),
        out_specs=whole(),
        out_shape=jax.ShapeDtypeStruct((CHUNK // NY, 1024), BF16),
        compiler_params=params(),
        name="project",
    )(place, *out, out_weight, near, far)


def solution(mesh):
    split = Mesh(mesh.devices.reshape(NZ, NX, NC, NY), ("z", "x", "c", "y"))
    rows = ("z", "x", "c")
    return jax.shard_map(
        per_device,
        mesh=split,
        in_specs=(P(rows, "y"), P(rows, "y"), P(rows, "y"), P("y", None)),
        out_specs=P((*rows, "y"), None),
        check_vma=False,
    )
```

```python
import functools
import math

import jax
import jax.numpy as jnp
from jax import lax
from jax.experimental import pallas as pl
from jax.experimental.pallas import tpu as pltpu
from jax.sharding import Mesh, PartitionSpec as P

HEAD_DIM = 64
F32 = jnp.float32
BF16 = jnp.bfloat16
MATMUL = (((1,), (0,)), ((), ()))

NZ, NX, NC, NY = 8, 4, 2, 4
CHUNK = 384
COLS = NX * CHUNK
SPAN = NC * CHUNK
WIDE = COLS // 2
VROWS = 80
LIMIT = 90.0
VMEM_LIMIT = 40 << 20


def whole():
    return pl.BlockSpec(memory_space=pltpu.VMEM)


def scalars():
    return pl.BlockSpec(memory_space=pltpu.SMEM)


def anywhere():
    return pl.BlockSpec(memory_space=pl.ANY)


def in_hbm():
    return pl.BlockSpec(memory_space=pltpu.HBM)


def split_kernel(place, k_hbm, v_hbm, q_hbm, *refs):
    outs, (k_ref, v_ref, q_ref, sems) = refs[: 2 * NX], refs[2 * NX :]
    pairs = ((k_hbm, k_ref), (v_hbm, v_ref), (q_hbm, q_ref))
    copies = [pltpu.make_async_copy(src, dst, sems.at[i]) for i, (src, dst) in enumerate(pairs)]
    for copy in copies:
        copy.start()
    for copy in copies:
        copy.wait()
    shift = lax.rem(COLS - HEAD_DIM * place[1], NX * HEAD_DIM)
    k, v, q = (pltpu.roll(r[...].astype(F32), shift, 1) for r in (k_ref, v_ref, q_ref))
    for d in range(NX):
        cols = slice(d * HEAD_DIM, (d + 1) * HEAD_DIM)
        outs[d][...] = jnp.concatenate([k[:, cols], v[:, cols]], axis=1).astype(BF16)
        rows = q[:, cols]
        outs[NX + d][...] = jnp.concatenate([rows[: CHUNK // 2], rows[CHUNK // 2 :]], axis=1).astype(BF16)


def queries_kernel(*refs):
    for d in range(NX):
        q = refs[d][...].astype(F32)
        q = jnp.concatenate([q[:, :HEAD_DIM], q[:, HEAD_DIM:]], axis=0) * (math.log2(math.e) / math.sqrt(HEAD_DIM))
        high = q.astype(BF16).astype(F32)
        both = jnp.concatenate([high, q - high], axis=1)
        refs[NX][:, d * CHUNK : (d + 1) * CHUNK] = both.T.astype(BF16)


def load_keys(kv, rows, k2, vt, kmax):
    keys, values = kv[:, :HEAD_DIM], kv[:, HEAD_DIM:]
    twice = jnp.concatenate([keys, keys], axis=1)
    k2[:rows, :] = twice
    vt[:HEAD_DIM, :rows] = values.T
    vt[HEAD_DIM:, :rows] = jnp.ones((VROWS - HEAD_DIM, rows), BF16)
    largest = jnp.max(jnp.abs(twice.astype(F32)).reshape(rows // 8, 8, 128), axis=0)
    kmax[...] = jnp.maximum(kmax[...], largest)


def segment(place, d):
    return lax.rem(place[1] - d + NX, NX)


def owner(place, half):
    return place[0] if half == 0 else NZ - 1 - place[0]


def source(place, step, other):
    ahead = (place[2] == 1) != other
    return lax.rem(place[0] + jnp.where(ahead, step, NZ - step), NZ)


def all_before(rows, half, q2, k2, vt, acc):
    cols = slice(half * WIDE, (half + 1) * WIDE)

    def body(i, carry):
        qb = q2[:, cols]
        total = acc[:, cols]
        for j in range(2):
            part = pl.ds(pl.multiple_of((2 * i + j) * WIDE, WIDE), WIDE)
            s = lax.dot_general(k2[part, :], qb, MATMUL, preferred_element_type=F32)
            weights = jnp.exp2(s).astype(BF16)
            total = total + lax.dot_general(vt[:, part], weights, MATMUL, preferred_element_type=F32)
        acc[:, cols] = total
        return carry

    lax.fori_loop(0, rows // WIDE // 2, body, 0)


def diagonal(place, rows, half, first, q2, k2, vt, acc):
    ahead = lax.broadcasted_iota(jnp.int32, (CHUNK, CHUNK), 0) - lax.broadcasted_iota(jnp.int32, (CHUNK, CHUNK), 1)

    def body(i, carry):
        d = NX // 2 * half + lax.rem(i, NX // 2)
        parity = jnp.where(i < NX // 2, first, 1 - first)
        cols = pl.ds(pl.multiple_of(d * CHUNK, CHUNK), CHUNK)
        part = pl.ds(pl.multiple_of((i // (NX // 2)) * COLS, COLS), COLS)
        s = lax.dot_general(k2[part, :], q2[:, cols], MATMUL, preferred_element_type=F32)
        parts = []
        for e in range(NX):
            far = SPAN * (segment(place, d) - segment(place, e)) + CHUNK * (place[2] - parity)
            w = jnp.exp2(s[e * CHUNK : (e + 1) * CHUNK])
            parts.append(jnp.where(ahead <= far, w, 0.0).astype(BF16))
        weights = jnp.concatenate(parts, axis=0)
        acc[:, cols] += lax.dot_general(vt[:, part], weights, MATMUL, preferred_element_type=F32)
        return carry

    lax.fori_loop(0, NX // 2 * (rows // COLS), body, 0)


def add_block(step, other, place, block, q2, acc, kmax, k2, vt):
    zk = source(place, step, other)
    rows = block.shape[0]

    @pl.when(jnp.logical_or(zk <= owner(place, 0), zk <= owner(place, 1)))
    def _():
        load_keys(block[...], rows, k2, vt, kmax)

    for half in range(2):

        @pl.when(zk < owner(place, half))
        def _(half=half):
            all_before(rows, half, q2, k2, vt, acc)

        if (step == 0 and half == 0) or (step % 2 == 1 and half == 1):

            @pl.when(zk == owner(place, half))
            def _(half=half):
                first = 1 - place[2] if other else place[2]
                diagonal(place, rows, half, first, q2, k2, vt, acc)


def step_kernel(step, other, place, q2, block, acc_in, kmax_in, acc, kmax, k2, vt):
    acc[...] = acc_in[...]
    kmax[...] = kmax_in[...]
    add_block(step, other, place, block, q2, acc, kmax, k2, vt)


def first_kernel(place, q2, own, other, acc, kmax, k2, vt):
    acc[...] = jnp.zeros_like(acc)
    kmax[...] = jnp.zeros_like(kmax)
    add_block(0, False, place, own, q2, acc, kmax, k2, vt)
    add_block(0, True, place, other, q2, acc, kmax, k2, vt)


def in_range(q2, kmax):
    most = jnp.broadcast_to(jnp.max(kmax[...], axis=0, keepdims=True), (8, 128)).astype(BF16)
    bound = lax.dot_general(most, jnp.abs(q2[...]), MATMUL, preferred_element_type=F32)
    return jnp.max(bound) <= LIMIT


def slow_block(place, zk, first, block, q2, acc, top, held, k2, vt, kmax, sem):
    ahead = lax.broadcasted_iota(jnp.int32, (CHUNK, CHUNK), 0) - lax.broadcasted_iota(jnp.int32, (CHUNK, CHUNK), 1)

    def one(e, carry):
        copy = pltpu.make_async_copy(block.at[pl.ds(pl.multiple_of(e * CHUNK, CHUNK), CHUNK)], held, sem)
        copy.start()
        copy.wait()
        load_keys(held[...], CHUNK, k2, vt, kmax)
        parity = jnp.where(e < NX, first, 1 - first)

        def body(d, carry):
            far = (
                NX * SPAN * (jnp.where(d < NX // 2, owner(place, 0), owner(place, 1)) - zk)
                + SPAN * (segment(place, d) - segment(place, lax.rem(e, NX)))
                + CHUNK * (place[2] - parity)
            )
            cols = pl.ds(pl.multiple_of(d * CHUNK, CHUNK), CHUNK)
            s = lax.dot_general(k2[:CHUNK, :], q2[:, cols], MATMUL, preferred_element_type=F32)
            keep = ahead <= far
            old = top[:1, cols]
            new = jnp.maximum(old, jnp.max(jnp.where(keep, s, -1e30), axis=0, keepdims=True))
            weights = jnp.where(keep, jnp.exp2(s - new), 0.0).astype(BF16)
            acc[:, cols] = acc[:, cols] * jnp.exp2(old - new) + lax.dot_general(
                vt[:, :CHUNK], weights, MATMUL, preferred_element_type=F32
            )
            top[:, cols] = jnp.broadcast_to(new, (8, CHUNK))
            return carry

        return lax.fori_loop(0, NX, body, carry)

    lax.fori_loop(0, block.shape[0] // CHUNK, one, 0)


def last_kernel(entries, place, q2, *refs):
    count = len(entries)
    blocks, kept = refs[:2], refs[2 : 2 + count]
    acc_in, kmax_in, *outs = refs[2 + count : 6 + count]
    acc, kmax, k2, vt, top, held, sem = refs[6 + count :]
    acc[...] = acc_in[...]
    kmax[...] = kmax_in[...]
    for block, (step, other) in zip(blocks, entries[-2:]):
        add_block(step, other, place, block, q2, acc, kmax, k2, vt)

    @pl.when(jnp.logical_not(in_range(q2, kmax)))
    def _():
        acc[...] = jnp.zeros_like(acc)
        top[...] = jnp.full(top.shape, -1e30, F32)
        for block, (step, other) in zip(kept, entries):
            first = 1 - place[2] if other else place[2]
            slow_block(place, source(place, step, other), first, block, q2, acc, top, held, k2, vt, kmax, sem)

    mixed = (acc[:HEAD_DIM, :] / acc[HEAD_DIM : HEAD_DIM + 1, :]).T
    for d in range(NX):
        part = mixed[d * CHUNK : (d + 1) * CHUNK].reshape(NY, 2, CHUNK // NY // 2, HEAD_DIM)
        outs[d // 2][d % 2] = jnp.concatenate([part[:, 0], part[:, 1]], axis=-1).astype(BF16)


def arrange_kernel(place, here, back, o_ref):
    for d in range(NX):
        o_ref[pl.ds(segment(place, d), 1)] = (here if d < 2 else back)[d % 2 : d % 2 + 1]


def project_kernel(place, r_ref, own, near, far, o_ref):
    lane = lax.broadcasted_iota(jnp.int32, (CHUNK // NY // 2, 128), 1) < HEAD_DIM
    even = place[2] == 0
    upper = lower = 0.0
    for e in range(NY):
        y = lax.rem(place[3] - e + NY, NY)
        left, right = [], []
        for x in range(0, NX, 2):
            a = r_ref[pl.ds(x * NY + y, 1)][0].astype(F32)
            b = r_ref[pl.ds((x + 1) * NY + y, 1)][0].astype(F32)
            left.append(jnp.where(lane, a, pltpu.roll(b, HEAD_DIM, 1)))
            right.append(jnp.where(lane, pltpu.roll(a, HEAD_DIM, 1), b))
        if e == 0:
            w = own[...]
        else:
            left, right = ([jnp.where(even, *p), jnp.where(even, *p[::-1])] for p in (left, right))
            w = jnp.concatenate([near[(e - 1) * 128 : e * 128], far[(e - 1) * 128 : e * 128]], axis=0)
        upper += jnp.dot(jnp.concatenate(left, axis=1).astype(BF16), w, preferred_element_type=F32)
        lower += jnp.dot(jnp.concatenate(right, axis=1).astype(BF16), w, preferred_element_type=F32)
    o_ref[...] = jnp.concatenate([upper, lower], axis=0).astype(BF16)


STATE = [jax.ShapeDtypeStruct((VROWS, COLS), F32), jax.ShapeDtypeStruct((8, 128), F32)]


def room(rows):
    return [pltpu.VMEM((rows, 128), BF16), pltpu.VMEM((VROWS, rows), BF16)]


def params():
    return pltpu.CompilerParams(vmem_limit_bytes=VMEM_LIMIT)


def cost(keys):
    return pl.CostEstimate(flops=keys, bytes_accessed=keys, transcendentals=0)


def split_heads(place, key_rows, value_rows, queries):
    return pl.pallas_call(
        split_kernel,
        in_specs=[scalars()] + [in_hbm()] * 3,
        out_specs=[whole()] * (2 * NX),
        out_shape=[jax.ShapeDtypeStruct((CHUNK, 128), BF16)] * NX
        + [jax.ShapeDtypeStruct((CHUNK // 2, 128), BF16)] * NX,
        scratch_shapes=[pltpu.VMEM((CHUNK, NX * HEAD_DIM), BF16)] * 3 + [pltpu.SemaphoreType.DMA((3,))],
        compiler_params=pltpu.CompilerParams(vmem_limit_bytes=60 << 20),
        name="split_heads",
    )(place, key_rows, value_rows, queries)


def scale_queries(q):
    return pl.pallas_call(
        queries_kernel,
        out_shape=jax.ShapeDtypeStruct((128, COLS), BF16),
        compiler_params=params(),
        name="scale_queries",
    )(*q)


def first_step(place, q2, own, other):
    return pl.pallas_call(
        first_kernel,
        in_specs=[scalars(), whole(), whole(), whole()],
        out_specs=[whole(), whole()],
        out_shape=STATE,
        scratch_shapes=room(own.shape[0]),
        compiler_params=params(),
        cost_estimate=cost(COLS),
        name="own_block",
    )(place, q2, own, other)


def next_step(place, q2, block, state, step, other):
    return pl.pallas_call(
        functools.partial(step_kernel, step, other),
        in_specs=[scalars()] + [whole()] * 4,
        out_specs=[whole(), whole()],
        out_shape=STATE,
        input_output_aliases={3: 0, 4: 1},
        scratch_shapes=room(block.shape[0]),
        compiler_params=params(),
        cost_estimate=cost(COLS),
        name="block_%d_%d" % (step, other),
    )(place, q2, block, *state)


def last_step(place, q2, blocks, state, kept, entries):
    return pl.pallas_call(
        functools.partial(last_kernel, entries),
        in_specs=[scalars()] + [whole()] * 3 + [anywhere()] * len(kept) + [whole()] * 2,
        out_specs=[whole()] * 2,
        out_shape=[jax.ShapeDtypeStruct((2, NY, CHUNK // NY // 2, 128), BF16)] * 2,
        scratch_shapes=[
            pltpu.VMEM((VROWS, COLS), F32),
            pltpu.VMEM((8, 128), F32),
            *room(blocks[0].shape[0]),
            pltpu.VMEM((8, COLS), F32),
            pltpu.VMEM((CHUNK, 128), BF16),
            pltpu.SemaphoreType.DMA,
        ],
        compiler_params=params(),
        cost_estimate=cost(COLS),
        name="last_block",
    )(place, q2, *blocks, *kept, *state)


def move(a, axis, size, by):
    return lax.ppermute(a, axis, [(i, (i + by) % size) for i in range(size)])


def move_ring(a):
    pairs = [(z * NC + c, (z + 1 - 2 * c) % NZ * NC + c) for z in range(NZ) for c in range(NC)]
    return lax.ppermute(a, ("z", "c"), pairs)


def mirror(a):
    return lax.ppermute(a, "z", [(z, NZ - 1 - z) for z in range(NZ)])


def move_segment(a, d):
    if d < NX // 2:
        return move(a, "x", NX, d)
    pairs = [(z * NX + x, (NZ - 1 - z) * NX + (x + d) % NX) for z in range(NZ) for x in range(NX)]
    return lax.ppermute(a, ("z", "x"), pairs)


def per_device(queries, key_rows, value_rows, out_weight):
    place = jnp.stack([lax.axis_index(a) for a in ("z", "x", "c", "y")]).astype(jnp.int32)
    pieces = split_heads(place, key_rows, value_rows, queries)
    q = pieces[NX:]
    own = jnp.concatenate([pieces[0]] + [move(pieces[d], "x", NX, d) for d in range(1, NX)], axis=0)
    own, q = lax.optimization_barrier((own, q))
    other = move(own, "c", NC, 1)
    first = move_ring(own)
    q2 = scale_queries([q[0]] + [move_segment(q[d], d) for d in range(1, NX)])
    other, out_weight = lax.optimization_barrier((other, out_weight))
    half = out_weight.shape[0] // NC
    quarter = half // 2
    mine = lax.dynamic_slice_in_dim(out_weight, place[2] * half, half, 0)
    after, before = move(mine, "y", NY, 1), move(mine, "y", NY, -1)
    state = first_step(place, q2, own, other)
    kept, entries = [own, other], [(0, False), (0, True)]
    block = jnp.concatenate([first, move_ring(other)], axis=0)
    block, state, after, before = lax.optimization_barrier((block, state, after, before))
    other = None
    for t in range(1, NZ // 2):
        late, other = other, move(block, "c", NC, 1)
        kept += [block, other]
        entries += [(t, False), (t, True)]
        if t == 1:
            across = [move(after[:quarter], "y", NY, 1), move(before[quarter:], "y", NY, -1)]
        if t == 2:
            near = jnp.concatenate([after, *across, before], axis=0)
            far = move(near, "c", NC, 1)
        state = next_step(place, q2, block, state, t, False)
        if t > 1:
            state = next_step(place, q2, late, state, t - 1, True)
        block = move_ring(block if t < NZ // 2 - 1 else block[:COLS])
        if t == 1:
            block, state, across = lax.optimization_barrier((block, state, across))
        elif t == 3:
            block, state, near, far = lax.optimization_barrier((block, state, near, far))
        else:
            block, state = lax.optimization_barrier((block, state))
    t = NZ // 2
    final = move(block, "c", NC, 1)
    state = next_step(place, q2, other, state, t - 1, True)
    kept += [block, final]
    entries += [(t, False), (t, True)]
    here, away = last_step(place, q2, [block, final], state, kept, tuple(entries))
    shape = (NX, *here.shape[1:])
    out = pl.pallas_call(
        arrange_kernel,
        in_specs=[scalars(), whole(), whole()],
        out_specs=whole(),
        out_shape=jax.ShapeDtypeStruct(shape, BF16),
        name="arrange",
    )(place, here, mirror(away))
    out = lax.all_to_all(out.reshape(NX * NY, *shape[2:]), ("x", "y"), 0, 0, tiled=True)
    return pl.pallas_call(
        project_kernel,
        in_specs=[scalars()] + [whole()] * 4,
        out_specs=whole(),
        out_shape=jax.ShapeDtypeStruct((CHUNK // NY, 1024), BF16),
        compiler_params=params(),
        name="project",
    )(place, out, out_weight, near, far)


def solution(mesh):
    split = Mesh(mesh.devices.reshape(NZ, NX, NC, NY), ("z", "x", "c", "y"))
    rows = ("z", "x", "c")
    return jax.shard_map(
        per_device,
        mesh=split,
        in_specs=(P(rows, "y"), P(rows, "y"), P(rows, "y"), P("y", None)),
        out_specs=P((*rows, "y"), None),
        check_vma=False,
    )
```

```python
import functools
import math

import jax
import jax.numpy as jnp
from jax import lax
from jax.experimental import pallas as pl
from jax.experimental.pallas import tpu as pltpu
from jax.sharding import Mesh, PartitionSpec as P

HEAD_DIM = 64
F32 = jnp.float32
BF16 = jnp.bfloat16
MATMUL = (((1,), (0,)), ((), ()))

NZ, NX, NC, NY = 8, 4, 2, 4
CHUNK = 384
COLS = NX * CHUNK
SPAN = NC * CHUNK
WIDE = COLS // 2
VROWS = 80
LIMIT = 90.0
VMEM_LIMIT = 40 << 20


def whole():
    return pl.BlockSpec(memory_space=pltpu.VMEM)


def scalars():
    return pl.BlockSpec(memory_space=pltpu.SMEM)


def anywhere():
    return pl.BlockSpec(memory_space=pl.ANY)


def in_hbm():
    return pl.BlockSpec(memory_space=pltpu.HBM)


def split_kernel(k_hbm, v_hbm, q_hbm, *refs):
    outs, (k_ref, v_ref, q_ref, sems) = refs[: 2 * NX], refs[2 * NX :]
    pairs = ((k_hbm, k_ref), (v_hbm, v_ref), (q_hbm, q_ref))
    copies = [pltpu.make_async_copy(src, dst, sems.at[i]) for i, (src, dst) in enumerate(pairs)]
    for copy in copies:
        copy.start()
    for copy in copies:
        copy.wait()
    shift = lax.rem(COLS - HEAD_DIM * lax.axis_index("x"), NX * HEAD_DIM)
    k, v, q = (pltpu.roll(r[...].astype(F32), shift, 1) for r in (k_ref, v_ref, q_ref))
    for d in range(NX):
        cols = slice(d * HEAD_DIM, (d + 1) * HEAD_DIM)
        outs[d][...] = jnp.concatenate([k[:, cols], v[:, cols]], axis=1).astype(BF16)
        rows = q[:, cols]
        outs[NX + d][...] = jnp.concatenate([rows[: CHUNK // 2], rows[CHUNK // 2 :]], axis=1).astype(BF16)


def queries_kernel(*refs):
    for d in range(NX):
        q = refs[d][...].astype(F32)
        q = jnp.concatenate([q[:, :HEAD_DIM], q[:, HEAD_DIM:]], axis=0) * (math.log2(math.e) / math.sqrt(HEAD_DIM))
        high = q.astype(BF16).astype(F32)
        both = jnp.concatenate([high, q - high], axis=1)
        refs[NX][:, d * CHUNK : (d + 1) * CHUNK] = both.T.astype(BF16)


def load_keys(kv, rows, k2, vt, kmax):
    keys, values = kv[:, :HEAD_DIM], kv[:, HEAD_DIM:]
    twice = jnp.concatenate([keys, keys], axis=1)
    k2[:rows, :] = twice
    vt[:HEAD_DIM, :rows] = values.T
    vt[HEAD_DIM:, :rows] = jnp.ones((VROWS - HEAD_DIM, rows), BF16)
    largest = jnp.max(jnp.abs(twice.astype(F32)).reshape(rows // 8, 8, 128), axis=0)
    kmax[...] = jnp.maximum(kmax[...], largest)


def segment(place, d):
    return lax.rem(place[1] - d + NX, NX)


def owner(place, half):
    return place[0] if half == 0 else NZ - 1 - place[0]


def source(place, step, other):
    ahead = (place[2] == 1) != other
    return lax.rem(place[0] + jnp.where(ahead, step, NZ - step), NZ)


def all_before(rows, half, q2, k2, vt, acc):
    cols = slice(half * WIDE, (half + 1) * WIDE)

    def body(i, carry):
        qb = q2[:, cols]
        total = acc[:, cols]
        for j in range(2):
            part = pl.ds(pl.multiple_of((2 * i + j) * WIDE, WIDE), WIDE)
            s = lax.dot_general(k2[part, :], qb, MATMUL, preferred_element_type=F32)
            weights = jnp.exp2(s).astype(BF16)
            total = total + lax.dot_general(vt[:, part], weights, MATMUL, preferred_element_type=F32)
        acc[:, cols] = total
        return carry

    lax.fori_loop(0, rows // WIDE // 2, body, 0)


def diagonal(place, rows, half, first, q2, k2, vt, acc):
    ahead = lax.broadcasted_iota(jnp.int32, (CHUNK, CHUNK), 0) - lax.broadcasted_iota(jnp.int32, (CHUNK, CHUNK), 1)

    def body(i, carry):
        d = NX // 2 * half + lax.rem(i, NX // 2)
        parity = jnp.where(i < NX // 2, first, 1 - first)
        cols = pl.ds(pl.multiple_of(d * CHUNK, CHUNK), CHUNK)
        part = pl.ds(pl.multiple_of((i // (NX // 2)) * COLS, COLS), COLS)
        s = lax.dot_general(k2[part, :], q2[:, cols], MATMUL, preferred_element_type=F32)
        parts = []
        for e in range(NX):
            far = SPAN * (segment(place, d) - segment(place, e)) + CHUNK * (place[2] - parity)
            w = jnp.exp2(s[e * CHUNK : (e + 1) * CHUNK])
            parts.append(jnp.where(ahead <= far, w, 0.0).astype(BF16))
        weights = jnp.concatenate(parts, axis=0)
        acc[:, cols] += lax.dot_general(vt[:, part], weights, MATMUL, preferred_element_type=F32)
        return carry

    lax.fori_loop(0, NX // 2 * (rows // COLS), body, 0)


def add_block(step, other, place, block, q2, acc, kmax, k2, vt):
    zk = source(place, step, other)
    rows = block.shape[0]

    @pl.when(jnp.logical_or(zk <= owner(place, 0), zk <= owner(place, 1)))
    def _():
        load_keys(block[...], rows, k2, vt, kmax)

    for half in range(2):

        @pl.when(zk < owner(place, half))
        def _(half=half):
            all_before(rows, half, q2, k2, vt, acc)

        if (step == 0 and half == 0) or (step % 2 == 1 and half == 1):

            @pl.when(zk == owner(place, half))
            def _(half=half):
                first = 1 - place[2] if other else place[2]
                diagonal(place, rows, half, first, q2, k2, vt, acc)


def step_kernel(step, other, place, q2, block, acc_in, kmax_in, acc, kmax, k2, vt):
    acc[...] = acc_in[...]
    kmax[...] = kmax_in[...]
    add_block(step, other, place, block, q2, acc, kmax, k2, vt)


def first_kernel(place, q2, own, other, acc, kmax, k2, vt):
    acc[...] = jnp.zeros_like(acc)
    kmax[...] = jnp.zeros_like(kmax)
    add_block(0, False, place, own, q2, acc, kmax, k2, vt)
    add_block(0, True, place, other, q2, acc, kmax, k2, vt)


def in_range(q2, kmax):
    most = jnp.broadcast_to(jnp.max(kmax[...], axis=0, keepdims=True), (8, 128)).astype(BF16)
    bound = lax.dot_general(most, jnp.abs(q2[...]), MATMUL, preferred_element_type=F32)
    return jnp.max(bound) <= LIMIT


def slow_block(place, zk, first, block, q2, acc, top, held, k2, vt, kmax, sem):
    ahead = lax.broadcasted_iota(jnp.int32, (CHUNK, CHUNK), 0) - lax.broadcasted_iota(jnp.int32, (CHUNK, CHUNK), 1)

    def one(e, carry):
        copy = pltpu.make_async_copy(block.at[pl.ds(pl.multiple_of(e * CHUNK, CHUNK), CHUNK)], held, sem)
        copy.start()
        copy.wait()
        load_keys(held[...], CHUNK, k2, vt, kmax)
        parity = jnp.where(e < NX, first, 1 - first)

        def body(d, carry):
            far = (
                NX * SPAN * (jnp.where(d < NX // 2, owner(place, 0), owner(place, 1)) - zk)
                + SPAN * (segment(place, d) - segment(place, lax.rem(e, NX)))
                + CHUNK * (place[2] - parity)
            )
            cols = pl.ds(pl.multiple_of(d * CHUNK, CHUNK), CHUNK)
            s = lax.dot_general(k2[:CHUNK, :], q2[:, cols], MATMUL, preferred_element_type=F32)
            keep = ahead <= far
            old = top[:1, cols]
            new = jnp.maximum(old, jnp.max(jnp.where(keep, s, -1e30), axis=0, keepdims=True))
            weights = jnp.where(keep, jnp.exp2(s - new), 0.0).astype(BF16)
            acc[:, cols] = acc[:, cols] * jnp.exp2(old - new) + lax.dot_general(
                vt[:, :CHUNK], weights, MATMUL, preferred_element_type=F32
            )
            top[:, cols] = jnp.broadcast_to(new, (8, CHUNK))
            return carry

        return lax.fori_loop(0, NX, body, carry)

    lax.fori_loop(0, block.shape[0] // CHUNK, one, 0)


def last_kernel(entries, place, q2, *refs):
    count = len(entries)
    block, kept = refs[0], refs[1 : 1 + count]
    acc_in, kmax_in, *outs = refs[1 + count : 3 + count + NX]
    acc, kmax, k2, vt, top, held, sem = refs[3 + count + NX :]
    acc[...] = acc_in[...]
    kmax[...] = kmax_in[...]
    add_block(*entries[-1], place, block, q2, acc, kmax, k2, vt)

    @pl.when(jnp.logical_not(in_range(q2, kmax)))
    def _():
        acc[...] = jnp.zeros_like(acc)
        top[...] = jnp.full(top.shape, -1e30, F32)
        for block, (step, other) in zip(kept, entries):
            first = 1 - place[2] if other else place[2]
            slow_block(place, source(place, step, other), first, block, q2, acc, top, held, k2, vt, kmax, sem)

    mixed = (acc[:HEAD_DIM, :] / acc[HEAD_DIM : HEAD_DIM + 1, :]).T
    for d in range(NX):
        part = mixed[d * CHUNK : (d + 1) * CHUNK].reshape(NY, 2, CHUNK // NY // 2, HEAD_DIM)
        both = jnp.concatenate([part[:, 0], part[:, 1]], axis=-1).astype(BF16)
        for y in range(NY):
            outs[d][pl.ds(lax.rem(y - place[3] + NY, NY), 1)] = both[y : y + 1]


def project_kernel(place, *refs):
    own, near, far, o_ref = refs[NY:]
    lane = lax.broadcasted_iota(jnp.int32, (CHUNK // NY // 2, 128), 1) < HEAD_DIM
    even = place[2] == 0
    upper = lower = 0.0
    for e in range(NY):
        left, right = [], []
        for x in range(0, NX, 2):
            a = refs[e][pl.ds(lax.rem(x - place[1] + NX, NX), 1)][0].astype(F32)
            b = refs[e][pl.ds(lax.rem(x + 1 - place[1] + NX, NX), 1)][0].astype(F32)
            left.append(jnp.where(lane, a, pltpu.roll(b, HEAD_DIM, 1)))
            right.append(jnp.where(lane, pltpu.roll(a, HEAD_DIM, 1), b))
        if e == 0:
            w = own[...]
        else:
            left, right = ([jnp.where(even, *p), jnp.where(even, *p[::-1])] for p in (left, right))
            w = jnp.concatenate([near[(e - 1) * 128 : e * 128], far[(e - 1) * 128 : e * 128]], axis=0)
        upper += jnp.dot(jnp.concatenate(left, axis=1).astype(BF16), w, preferred_element_type=F32)
        lower += jnp.dot(jnp.concatenate(right, axis=1).astype(BF16), w, preferred_element_type=F32)
    o_ref[...] = jnp.concatenate([upper, lower], axis=0).astype(BF16)


STATE = [jax.ShapeDtypeStruct((VROWS, COLS), F32), jax.ShapeDtypeStruct((8, 128), F32)]


def room(rows):
    return [pltpu.VMEM((rows, 128), BF16), pltpu.VMEM((VROWS, rows), BF16)]


def params():
    return pltpu.CompilerParams(vmem_limit_bytes=VMEM_LIMIT)


def cost(keys):
    return pl.CostEstimate(flops=keys, bytes_accessed=keys, transcendentals=0)


def split_heads(key_rows, value_rows, queries):
    return pl.pallas_call(
        split_kernel,
        in_specs=[in_hbm()] * 3,
        out_specs=[whole()] * (2 * NX),
        out_shape=[jax.ShapeDtypeStruct((CHUNK, 128), BF16)] * NX
        + [jax.ShapeDtypeStruct((CHUNK // 2, 128), BF16)] * NX,
        scratch_shapes=[pltpu.VMEM((CHUNK, NX * HEAD_DIM), BF16)] * 3 + [pltpu.SemaphoreType.DMA((3,))],
        compiler_params=pltpu.CompilerParams(vmem_limit_bytes=60 << 20),
        name="split_heads",
    )(key_rows, value_rows, queries)


def scale_queries(q):
    return pl.pallas_call(
        queries_kernel,
        out_shape=jax.ShapeDtypeStruct((128, COLS), BF16),
        compiler_params=params(),
        name="scale_queries",
    )(*q)


def first_step(place, q2, own, other):
    return pl.pallas_call(
        first_kernel,
        in_specs=[scalars(), whole(), whole(), whole()],
        out_specs=[whole(), whole()],
        out_shape=STATE,
        scratch_shapes=room(own.shape[0]),
        compiler_params=params(),
        cost_estimate=cost(COLS),
        name="own_block",
    )(place, q2, own, other)


def next_step(place, q2, block, state, step, other):
    return pl.pallas_call(
        functools.partial(step_kernel, step, other),
        in_specs=[scalars()] + [whole()] * 4,
        out_specs=[whole(), whole()],
        out_shape=STATE,
        input_output_aliases={3: 0, 4: 1},
        scratch_shapes=room(block.shape[0]),
        compiler_params=params(),
        cost_estimate=cost(COLS),
        name="block_%d_%d" % (step, other),
    )(place, q2, block, *state)


def last_step(place, q2, block, state, kept, entries):
    return pl.pallas_call(
        functools.partial(last_kernel, entries),
        in_specs=[scalars()] + [whole()] * 2 + [anywhere()] * len(kept) + [whole()] * 2,
        out_specs=[whole()] * NX,
        out_shape=[jax.ShapeDtypeStruct((NY, CHUNK // NY // 2, 128), BF16)] * NX,
        scratch_shapes=[
            pltpu.VMEM((VROWS, COLS), F32),
            pltpu.VMEM((8, 128), F32),
            *room(block.shape[0]),
            pltpu.VMEM((8, COLS), F32),
            pltpu.VMEM((CHUNK, 128), BF16),
            pltpu.SemaphoreType.DMA,
        ],
        compiler_params=params(),
        cost_estimate=cost(COLS),
        name="last_block",
    )(place, q2, block, *kept, *state)


def move(a, axis, size, by):
    return lax.ppermute(a, axis, [(i, (i + by) % size) for i in range(size)])


def move_ring(a):
    pairs = [(z * NC + c, (z + 1 - 2 * c) % NZ * NC + c) for z in range(NZ) for c in range(NC)]
    return lax.ppermute(a, ("z", "c"), pairs)


def move_segment(a, d, back):
    by = -d if back else d
    if d < NX // 2:
        return move(a, "x", NX, by)
    pairs = [(z * NX + x, (NZ - 1 - z) * NX + (x + by) % NX) for z in range(NZ) for x in range(NX)]
    return lax.ppermute(a, ("z", "x"), pairs)


def per_device(queries, key_rows, value_rows, out_weight):
    place = jnp.stack([lax.axis_index(a) for a in ("z", "x", "c", "y")]).astype(jnp.int32)
    pieces = split_heads(key_rows, value_rows, queries)
    q = [pieces[NX]] + [move_segment(pieces[NX + d], d, False) for d in range(1, NX)]
    own = jnp.concatenate([pieces[0]] + [move(pieces[d], "x", NX, d) for d in range(1, NX)], axis=0)
    own, q, out_weight = lax.optimization_barrier((own, q, out_weight))
    other = move(own, "c", NC, 1)
    first = move_ring(own)
    q2 = scale_queries(q)
    other, out_weight = lax.optimization_barrier((other, out_weight))
    half = out_weight.shape[0] // NC
    quarter = half // 2
    mine = lax.dynamic_slice_in_dim(out_weight, place[2] * half, half, 0)
    after, before = move(mine, "y", NY, 1), move(mine, "y", NY, -1)
    state = first_step(place, q2, own, other)
    kept, entries = [own, other], [(0, False), (0, True)]
    block = jnp.concatenate([first, move_ring(other)], axis=0)
    block, state, after, before = lax.optimization_barrier((block, state, after, before))
    for t in range(1, NZ // 2):
        other = move(block, "c", NC, 1)
        kept += [block, other]
        entries += [(t, False), (t, True)]
        state = next_step(place, q2, block, state, t, False)
        state = next_step(place, q2, other, state, t, True)
        block = move_ring(block if t < NZ // 2 - 1 else block[:COLS])
        if t == 1:
            across = [move(after[:quarter], "y", NY, 1), move(before[quarter:], "y", NY, -1)]
            block, state, across = lax.optimization_barrier((block, state, across))
            near = jnp.concatenate([after, *across, before], axis=0)
            far = move(near, "c", NC, 1)
        elif t == 3:
            block, state, near, far = lax.optimization_barrier((block, state, near, far))
        else:
            block, state = lax.optimization_barrier((block, state))
    t = NZ // 2
    other = move(block, "c", NC, 1)
    kept += [block, other]
    entries += [(t, False), (t, True)]
    state = next_step(place, q2, block, state, t, False)
    out = last_step(place, q2, other, state, kept, tuple(entries))
    out = [out[0]] + [move_segment(out[d], d, True) for d in range(1, NX)]
    out = [jnp.stack([out[d][e] for d in range(NX)]) for e in range(NY)]
    out = [out[0]] + [move(out[e], "y", NY, e) for e in range(1, NY)]
    return pl.pallas_call(
        project_kernel,
        in_specs=[scalars()] + [whole()] * (NY + 3),
        out_specs=whole(),
        out_shape=jax.ShapeDtypeStruct((CHUNK // NY, 1024), BF16),
        compiler_params=params(),
        name="project",
    )(place, *out, out_weight, near, far)


def solution(mesh):
    split = Mesh(mesh.devices.reshape(NZ, NX, NC, NY), ("z", "x", "c", "y"))
    rows = ("z", "x", "c")
    return jax.shard_map(
        per_device,
        mesh=split,
        in_specs=(P(rows, "y"), P(rows, "y"), P(rows, "y"), P("y", None)),
        out_specs=P((*rows, "y"), None),
        check_vma=False,
    )
```

```python
import functools
import math

import jax
import jax.numpy as jnp
from jax import lax
from jax.experimental import pallas as pl
from jax.experimental.pallas import tpu as pltpu
from jax.sharding import Mesh, PartitionSpec as P

HEAD_DIM = 64
F32 = jnp.float32
BF16 = jnp.bfloat16
MATMUL = (((1,), (0,)), ((), ()))

NZ, NX, NC, NY = 8, 4, 2, 4
CHUNK = 384
COLS = NX * CHUNK
SPAN = NC * CHUNK
WIDE = COLS // 2
ROWS = CHUNK // NY // 2
VROWS = 80
LIMIT = 90.0
VMEM_LIMIT = 40 << 20


def whole():
    return pl.BlockSpec(memory_space=pltpu.VMEM)


def scalars():
    return pl.BlockSpec(memory_space=pltpu.SMEM)


def anywhere():
    return pl.BlockSpec(memory_space=pl.ANY)


def in_hbm():
    return pl.BlockSpec(memory_space=pltpu.HBM)


def split_kernel(k_hbm, v_hbm, q_hbm, *refs):
    outs, (k_ref, v_ref, q_ref, sems) = refs[: NX + 2], refs[NX + 2 :]
    pairs = ((k_hbm, k_ref), (v_hbm, v_ref), (q_hbm, q_ref))
    copies = [pltpu.make_async_copy(src, dst, sems.at[i]) for i, (src, dst) in enumerate(pairs)]
    for copy in copies:
        copy.start()
    for copy in copies:
        copy.wait()
    shift = lax.rem(COLS - HEAD_DIM * lax.axis_index("x"), NX * HEAD_DIM)
    k, v = (pltpu.roll(r[...].astype(F32), shift, 1) for r in (k_ref, v_ref))
    for d in range(NX):
        cols = slice(d * HEAD_DIM, (d + 1) * HEAD_DIM)
        outs[d][...] = jnp.concatenate([k[:, cols], v[:, cols]], axis=1).astype(BF16)
    for y in range(NY):
        for half in range(2):
            outs[NX + half][y * ROWS : (y + 1) * ROWS, :] = q_ref[pl.ds((2 * y + half) * ROWS, ROWS), :]


def pair_kernel(place, a_ref, b_ref, *outs):
    shift = lax.rem(COLS - HEAD_DIM * place[1], NX * HEAD_DIM)
    a, b = (pltpu.roll(r[...].astype(F32), shift, 1) for r in (a_ref, b_ref))
    for d in range(NX):
        cols = slice(d * HEAD_DIM, (d + 1) * HEAD_DIM)
        outs[d][...] = jnp.concatenate([a[:, cols], b[:, cols]], axis=1).astype(BF16)


def queries_kernel(*refs):
    for half in range(2):
        cols = slice(half * HEAD_DIM, (half + 1) * HEAD_DIM)
        q = jnp.concatenate([refs[d][...].astype(F32)[:, cols] for d in range(NX)], axis=0)
        q = q * (math.log2(math.e) / math.sqrt(HEAD_DIM))
        high = q.astype(BF16).astype(F32)
        both = jnp.concatenate([high, q - high], axis=1)
        refs[NX][:, half * WIDE : (half + 1) * WIDE] = both.T.astype(BF16)


def load_keys(kv, rows, k2, vt, kmax):
    keys, values = kv[:, :HEAD_DIM], kv[:, HEAD_DIM:]
    twice = jnp.concatenate([keys, keys], axis=1)
    k2[:rows, :] = twice
    vt[:HEAD_DIM, :rows] = values.T
    vt[HEAD_DIM:, :rows] = jnp.ones((VROWS - HEAD_DIM, rows), BF16)
    largest = jnp.max(jnp.abs(twice.astype(F32)).reshape(rows // 8, 8, 128), axis=0)
    kmax[...] = jnp.maximum(kmax[...], largest)


def segment(place, d):
    return lax.rem(place[1] - d + NX, NX)


def owner(place, half):
    return place[0] if half == 0 else NZ - 1 - place[0]


def source(place, step, other):
    ahead = (place[2] == 1) != other
    return lax.rem(place[0] + jnp.where(ahead, step, NZ - step), NZ)


def all_before(rows, half, q2, k2, vt, acc):
    cols = slice(half * WIDE, (half + 1) * WIDE)

    qb = q2[:, cols]
    total = acc[:, cols]
    for start in range(0, rows, WIDE):
        part = slice(start, start + WIDE)
        s = lax.dot_general(k2[part, :], qb, MATMUL, preferred_element_type=F32)
        weights = jnp.exp2(s).astype(BF16)
        total = total + lax.dot_general(vt[:, part], weights, MATMUL, preferred_element_type=F32)
    acc[:, cols] = total


def diagonal(place, rows, half, first, q2, qpos, k2, vt, acc):
    cols = slice(half * WIDE, (half + 1) * WIDE)
    row = lax.broadcasted_iota(jnp.int32, (CHUNK, WIDE), 0)

    def body(i, carry):
        parity = jnp.where(i == 0, first, 1 - first)
        part = pl.ds(pl.multiple_of(i * COLS, COLS), COLS)
        s = lax.dot_general(k2[part, :], q2[:, cols], MATMUL, preferred_element_type=F32)
        parts = []
        for e in range(NX):
            seen = qpos[:, cols] - (SPAN * segment(place, e) + CHUNK * parity)
            w = jnp.exp2(s[e * CHUNK : (e + 1) * CHUNK])
            parts.append(jnp.where(row <= seen, w, 0.0).astype(BF16))
        weights = jnp.concatenate(parts, axis=0)
        acc[:, cols] += lax.dot_general(vt[:, part], weights, MATMUL, preferred_element_type=F32)
        return carry

    lax.fori_loop(0, rows // COLS, body, 0)


def add_block(step, other, place, block, q2, qpos, acc, kmax, k2, vt):
    zk = source(place, step, other)
    rows = block.shape[0]

    @pl.when(jnp.logical_or(zk <= owner(place, 0), zk <= owner(place, 1)))
    def _():
        load_keys(block[...], rows, k2, vt, kmax)

    for half in range(2):

        @pl.when(zk < owner(place, half))
        def _(half=half):
            all_before(rows, half, q2, k2, vt, acc)

        if (step == 0 and half == 0) or (step % 2 == 1 and half == 1):

            @pl.when(zk == owner(place, half))
            def _(half=half):
                first = 1 - place[2] if other else place[2]
                diagonal(place, rows, half, first, q2, qpos, k2, vt, acc)


def step_kernel(step, other, place, q2, qpos, block, acc_in, kmax_in, acc, kmax, k2, vt):
    acc[...] = acc_in[...]
    kmax[...] = kmax_in[...]
    add_block(step, other, place, block, q2, qpos, acc, kmax, k2, vt)


def first_kernel(place, q2, qpos, own, other, acc, kmax, k2, vt):
    acc[...] = jnp.zeros_like(acc)
    kmax[...] = jnp.zeros_like(kmax)
    add_block(0, False, place, own, q2, qpos, acc, kmax, k2, vt)
    add_block(0, True, place, other, q2, qpos, acc, kmax, k2, vt)


def in_range(q2, kmax):
    most = jnp.broadcast_to(jnp.max(kmax[...], axis=0, keepdims=True), (8, 128)).astype(BF16)
    bound = lax.dot_general(most, jnp.abs(q2[...]), MATMUL, preferred_element_type=F32)
    return jnp.max(bound) <= LIMIT


def slow_block(place, zk, first, block, q2, qpos, acc, top, held, k2, vt, kmax, sem):
    row = lax.broadcasted_iota(jnp.int32, (CHUNK, CHUNK), 0)

    def one(e, carry):
        copy = pltpu.make_async_copy(block.at[pl.ds(pl.multiple_of(e * CHUNK, CHUNK), CHUNK)], held, sem)
        copy.start()
        copy.wait()
        load_keys(held[...], CHUNK, k2, vt, kmax)
        parity = jnp.where(e < NX, first, 1 - first)

        def body(d, carry):
            ahead = NX * SPAN * (jnp.where(d < NX // 2, owner(place, 0), owner(place, 1)) - zk)
            base = SPAN * segment(place, lax.rem(e, NX)) + CHUNK * parity
            cols = pl.ds(pl.multiple_of(d * CHUNK, CHUNK), CHUNK)
            s = lax.dot_general(k2[:CHUNK, :], q2[:, cols], MATMUL, preferred_element_type=F32)
            keep = row <= qpos[:, cols] + (ahead - base)
            old = top[:1, cols]
            new = jnp.maximum(old, jnp.max(jnp.where(keep, s, -1e30), axis=0, keepdims=True))
            weights = jnp.where(keep, jnp.exp2(s - new), 0.0).astype(BF16)
            acc[:, cols] = acc[:, cols] * jnp.exp2(old - new) + lax.dot_general(
                vt[:, :CHUNK], weights, MATMUL, preferred_element_type=F32
            )
            top[:, cols] = jnp.broadcast_to(new, (8, CHUNK))
            return carry

        return lax.fori_loop(0, NX, body, carry)

    lax.fori_loop(0, block.shape[0] // CHUNK, one, 0)


def last_kernel(entries, place, q2, qpos, *refs):
    count = len(entries)
    block, kept = refs[0], refs[1 : 1 + count]
    acc_in, kmax_in, *outs = refs[1 + count : 3 + count + NX]
    acc, kmax, k2, vt, top, held, sem = refs[3 + count + NX :]
    acc[...] = acc_in[...]
    kmax[...] = kmax_in[...]
    add_block(*entries[-1], place, block, q2, qpos, acc, kmax, k2, vt)

    @pl.when(jnp.logical_not(in_range(q2, kmax)))
    def _():
        acc[...] = jnp.zeros_like(acc)
        top[...] = jnp.full(top.shape, -1e30, F32)
        for block, (step, other) in zip(kept, entries):
            first = 1 - place[2] if other else place[2]
            slow_block(place, source(place, step, other), first, block, q2, qpos, acc, top, held, k2, vt, kmax, sem)

    mixed = (acc[:HEAD_DIM, :] / acc[HEAD_DIM : HEAD_DIM + 1, :]).T
    mixed = mixed.reshape(2, NX, NY, ROWS, HEAD_DIM)
    for d in range(NX):
        both = jnp.concatenate([mixed[0, d], mixed[1, d]], axis=-1).astype(BF16)
        for y in range(NY):
            outs[d][pl.ds(lax.rem(y - place[3] + NY, NY), 1)] = both[y : y + 1]


def project_kernel(place, *refs):
    own, near, far, *outs = refs[NY:]
    lane = lax.broadcasted_iota(jnp.int32, (CHUNK // NY // 2, 128), 1) < HEAD_DIM
    even = place[2] == 0
    upper = lower = 0.0
    for e in range(NY):
        left, right = [], []
        for x in range(0, NX, 2):
            a = refs[e][pl.ds(lax.rem(x - place[1] + NX, NX), 1)][0].astype(F32)
            b = refs[e][pl.ds(lax.rem(x + 1 - place[1] + NX, NX), 1)][0].astype(F32)
            left.append(jnp.where(lane, a, pltpu.roll(b, HEAD_DIM, 1)))
            right.append(jnp.where(lane, pltpu.roll(a, HEAD_DIM, 1), b))
        if e == 0:
            w = own[...]
        else:
            left, right = ([jnp.where(even, *p), jnp.where(even, *p[::-1])] for p in (left, right))
            w = jnp.concatenate([near[(e - 1) * 128 : e * 128], far[(e - 1) * 128 : e * 128]], axis=0)
        upper += jnp.dot(jnp.concatenate(left, axis=1).astype(BF16), w, preferred_element_type=F32)
        lower += jnp.dot(jnp.concatenate(right, axis=1).astype(BF16), w, preferred_element_type=F32)
    outs[0][...] = upper.astype(BF16)
    outs[1][...] = lower.astype(BF16)


STATE = [jax.ShapeDtypeStruct((VROWS, COLS), F32), jax.ShapeDtypeStruct((8, 128), F32)]


def room(rows):
    return [pltpu.VMEM((rows, 128), BF16), pltpu.VMEM((VROWS, rows), BF16)]


def params():
    return pltpu.CompilerParams(vmem_limit_bytes=VMEM_LIMIT)


def cost(keys):
    return pl.CostEstimate(flops=keys, bytes_accessed=keys, transcendentals=0)


def split_heads(key_rows, value_rows, queries):
    return pl.pallas_call(
        split_kernel,
        in_specs=[in_hbm()] * 3,
        out_specs=[whole()] * (NX + 2),
        out_shape=[jax.ShapeDtypeStruct((CHUNK, 128), BF16)] * NX
        + [jax.ShapeDtypeStruct((CHUNK // 2, NX * HEAD_DIM), BF16)] * 2,
        scratch_shapes=[pltpu.VMEM((CHUNK, NX * HEAD_DIM), BF16)] * 3 + [pltpu.SemaphoreType.DMA((3,))],
        compiler_params=pltpu.CompilerParams(vmem_limit_bytes=60 << 20),
        name="split_heads",
    )(key_rows, value_rows, queries)


def pair_queries(place, here, there):
    return pl.pallas_call(
        pair_kernel,
        in_specs=[scalars(), whole(), whole()],
        out_specs=[whole()] * NX,
        out_shape=[jax.ShapeDtypeStruct((CHUNK // 2, 128), BF16)] * NX,
        compiler_params=params(),
        name="pair_queries",
    )(place, here, there)


def scale_queries(q):
    return pl.pallas_call(
        queries_kernel,
        out_shape=jax.ShapeDtypeStruct((128, COLS), BF16),
        compiler_params=params(),
        name="scale_queries",
    )(*q)


def first_step(place, q2, qpos, own, other):
    return pl.pallas_call(
        first_kernel,
        in_specs=[scalars()] + [whole()] * 4,
        out_specs=[whole(), whole()],
        out_shape=STATE,
        scratch_shapes=room(own.shape[0]),
        compiler_params=params(),
        cost_estimate=cost(COLS),
        name="own_block",
    )(place, q2, qpos, own, other)


def next_step(place, q2, qpos, block, state, step, other):
    return pl.pallas_call(
        functools.partial(step_kernel, step, other),
        in_specs=[scalars()] + [whole()] * 5,
        out_specs=[whole(), whole()],
        out_shape=STATE,
        input_output_aliases={4: 0, 5: 1},
        scratch_shapes=room(block.shape[0]),
        compiler_params=params(),
        cost_estimate=cost(COLS),
        name="block_%d_%d" % (step, other),
    )(place, q2, qpos, block, *state)


def last_step(place, q2, qpos, block, state, kept, entries):
    return pl.pallas_call(
        functools.partial(last_kernel, entries),
        in_specs=[scalars()] + [whole()] * 3 + [anywhere()] * len(kept) + [whole()] * 2,
        out_specs=[whole()] * NX,
        out_shape=[jax.ShapeDtypeStruct((NY, CHUNK // NY // 2, 128), BF16)] * NX,
        scratch_shapes=[
            pltpu.VMEM((VROWS, COLS), F32),
            pltpu.VMEM((8, 128), F32),
            *room(block.shape[0]),
            pltpu.VMEM((8, COLS), F32),
            pltpu.VMEM((CHUNK, 128), BF16),
            pltpu.SemaphoreType.DMA,
        ],
        compiler_params=params(),
        cost_estimate=cost(COLS),
        name="last_block",
    )(place, q2, qpos, block, *kept, *state)


def move(a, axis, size, by):
    return lax.ppermute(a, axis, [(i, (i + by) % size) for i in range(size)])


def move_ring(a):
    pairs = [(z * NC + c, (z + 1 - 2 * c) % NZ * NC + c) for z in range(NZ) for c in range(NC)]
    return lax.ppermute(a, ("z", "c"), pairs)


def mirror(a):
    return lax.ppermute(a, "z", [(z, NZ - 1 - z) for z in range(NZ)])


def query_positions(place):
    n = jnp.arange(COLS, dtype=jnp.int32).reshape(1, COLS)
    half, d, y, row = n // WIDE, n % WIDE // (NY * ROWS), n // ROWS % NY, n % ROWS
    return SPAN * ((place[1] - d + NX) % NX) + CHUNK * place[2] + ROWS * (2 * y + half) + row


def per_device(queries, key_rows, value_rows, out_weight):
    place = jnp.stack([lax.axis_index(a) for a in ("z", "x", "c", "y")]).astype(jnp.int32)
    *pieces, here, there = split_heads(key_rows, value_rows, queries)
    there = mirror(there)
    own = jnp.concatenate([pieces[0]] + [move(pieces[d], "x", NX, d) for d in range(1, NX)], axis=0)
    own, there, out_weight = lax.optimization_barrier((own, there, out_weight))
    other = move(own, "c", NC, 1)
    first = move_ring(own)
    q = pair_queries(place, here, there)
    q2 = scale_queries([q[0]] + [move(q[d], "x", NX, d) for d in range(1, NX)])
    qpos = query_positions(place)
    other, out_weight = lax.optimization_barrier((other, out_weight))
    half = out_weight.shape[0] // NC
    quarter = half // 2
    mine = lax.dynamic_slice_in_dim(out_weight, place[2] * half, half, 0)
    after, before = move(mine, "y", NY, 1), move(mine, "y", NY, -1)
    state = first_step(place, q2, qpos, own, other)
    kept, entries = [own, other], [(0, False), (0, True)]
    block = jnp.concatenate([first, move_ring(other)], axis=0)
    block, state, after, before = lax.optimization_barrier((block, state, after, before))
    for t in range(1, NZ // 2):
        other = move(block, "c", NC, 1)
        kept += [block, other]
        entries += [(t, False), (t, True)]
        state = next_step(place, q2, qpos, block, state, t, False)
        state = next_step(place, q2, qpos, other, state, t, True)
        block = move_ring(block if t < NZ // 2 - 1 else block[:COLS])
        if t == 1:
            across = [move(after[:quarter], "y", NY, 1), move(before[quarter:], "y", NY, -1)]
            block, state, across = lax.optimization_barrier((block, state, across))
            near = jnp.concatenate([after, *across, before], axis=0)
            far = move(near, "c", NC, 1)
        elif t == 3:
            block, state, near, far = lax.optimization_barrier((block, state, near, far))
        else:
            block, state = lax.optimization_barrier((block, state))
    t = NZ // 2
    other = move(block, "c", NC, 1)
    kept += [block, other]
    entries += [(t, False), (t, True)]
    state = next_step(place, q2, qpos, block, state, t, False)
    out = last_step(place, q2, qpos, other, state, kept, tuple(entries))
    out = [out[0]] + [move(out[d], "x", NX, -d) for d in range(1, NX)]
    out = [jnp.stack([out[d][e] for d in range(NX)]) for e in range(NY)]
    out = [out[0]] + [move(out[e], "y", NY, e) for e in range(1, NY)]
    here, there = pl.pallas_call(
        project_kernel,
        in_specs=[scalars()] + [whole()] * (NY + 3),
        out_specs=[whole()] * 2,
        out_shape=[jax.ShapeDtypeStruct((ROWS, 1024), BF16)] * 2,
        compiler_params=params(),
        name="project",
    )(place, *out, out_weight, near, far)
    return jnp.concatenate([here, mirror(there)], axis=0)


def solution(mesh):
    split = Mesh(mesh.devices.reshape(NZ, NX, NC, NY), ("z", "x", "c", "y"))
    rows = ("z", "x", "c")
    return jax.shard_map(
        per_device,
        mesh=split,
        in_specs=(P(rows, "y"), P(rows, "y"), P(rows, "y"), P("y", None)),
        out_specs=P((*rows, "y"), None),
        check_vma=False,
    )
```

```python
import functools
import math

import jax
import jax.numpy as jnp
from jax import lax
from jax.experimental import pallas as pl
from jax.experimental.pallas import tpu as pltpu
from jax.sharding import Mesh, PartitionSpec as P

HEAD_DIM = 64
F32 = jnp.float32
BF16 = jnp.bfloat16
MATMUL = (((1,), (0,)), ((), ()))

NZ, NX, NC, NY = 8, 4, 2, 4
CHUNK = 384
COLS = NX * CHUNK
SPAN = NC * CHUNK
WIDE = COLS // 2
ROWS = CHUNK // NY // 2
VROWS = 80
LIMIT = 90.0
VMEM_LIMIT = 40 << 20


def whole():
    return pl.BlockSpec(memory_space=pltpu.VMEM)


def scalars():
    return pl.BlockSpec(memory_space=pltpu.SMEM)


def anywhere():
    return pl.BlockSpec(memory_space=pl.ANY)


def in_hbm():
    return pl.BlockSpec(memory_space=pltpu.HBM)


def split_kernel(k_hbm, v_hbm, q_hbm, *refs):
    outs, (k_ref, v_ref, q_ref, sems) = refs[: NX + 2], refs[NX + 2 :]
    pairs = ((k_hbm, k_ref), (v_hbm, v_ref), (q_hbm, q_ref))
    copies = [pltpu.make_async_copy(src, dst, sems.at[i]) for i, (src, dst) in enumerate(pairs)]
    for copy in copies:
        copy.start()
    for copy in copies:
        copy.wait()
    shift = lax.rem(COLS - HEAD_DIM * lax.axis_index("x"), NX * HEAD_DIM)
    k, v = (pltpu.roll(r[...].astype(F32), shift, 1) for r in (k_ref, v_ref))
    for d in range(NX):
        cols = slice(d * HEAD_DIM, (d + 1) * HEAD_DIM)
        outs[d][...] = jnp.concatenate([k[:, cols], v[:, cols]], axis=1).astype(BF16)
    for y in range(NY):
        for half in range(2):
            outs[NX + half][y * ROWS : (y + 1) * ROWS, :] = q_ref[pl.ds((2 * y + half) * ROWS, ROWS), :]


def pair_kernel(place, a_ref, b_ref, *outs):
    shift = lax.rem(COLS - HEAD_DIM * place[1], NX * HEAD_DIM)
    a, b = (pltpu.roll(r[...].astype(F32), shift, 1) for r in (a_ref, b_ref))
    for d in range(NX):
        cols = slice(d * HEAD_DIM, (d + 1) * HEAD_DIM)
        outs[d][...] = jnp.concatenate([a[:, cols], b[:, cols]], axis=1).astype(BF16)


def queries_kernel(*refs):
    for half in range(2):
        cols = slice(half * HEAD_DIM, (half + 1) * HEAD_DIM)
        q = jnp.concatenate([refs[d][...].astype(F32)[:, cols] for d in range(NX)], axis=0)
        q = q * (math.log2(math.e) / math.sqrt(HEAD_DIM))
        high = q.astype(BF16).astype(F32)
        both = jnp.concatenate([high, q - high], axis=1)
        refs[NX][:, half * WIDE : (half + 1) * WIDE] = both.T.astype(BF16)


def load_keys(kv, rows, k2, vt, kmax):
    keys, values = kv[:, :HEAD_DIM], kv[:, HEAD_DIM:]
    twice = jnp.concatenate([keys, keys], axis=1)
    k2[:rows, :] = twice
    vt[:HEAD_DIM, :rows] = values.T
    vt[HEAD_DIM:, :rows] = jnp.ones((VROWS - HEAD_DIM, rows), BF16)
    largest = jnp.max(jnp.abs(twice.astype(F32)).reshape(rows // 8, 8, 128), axis=0)
    kmax[...] = jnp.maximum(kmax[...], largest)


def segment(place, d):
    return lax.rem(place[1] - d + NX, NX)


def owner(place, half):
    return place[0] if half == 0 else NZ - 1 - place[0]


def source(place, step, other):
    ahead = (place[2] == 1) != other
    return lax.rem(place[0] + jnp.where(ahead, step, NZ - step), NZ)


def all_before(rows, half, q2, k2, vt, acc):
    cols = slice(half * WIDE, (half + 1) * WIDE)

    qb = q2[:, cols]
    total = acc[:, cols]
    for start in range(0, rows, WIDE):
        part = slice(start, start + WIDE)
        s = lax.dot_general(k2[part, :], qb, MATMUL, preferred_element_type=F32)
        weights = jnp.exp2(s).astype(BF16)
        total = total + lax.dot_general(vt[:, part], weights, MATMUL, preferred_element_type=F32)
    acc[:, cols] = total


def diagonal(place, rows, half, first, q2, qpos, k2, vt, acc):
    cols = slice(half * WIDE, (half + 1) * WIDE)
    row = lax.broadcasted_iota(jnp.int32, (CHUNK, WIDE), 0)

    def body(i, carry):
        parity = jnp.where(i == 0, first, 1 - first)
        part = pl.ds(pl.multiple_of(i * COLS, COLS), COLS)
        s = lax.dot_general(k2[part, :], q2[:, cols], MATMUL, preferred_element_type=F32)
        parts = []
        for e in range(NX):
            seen = qpos[:, cols] - (SPAN * segment(place, e) + CHUNK * parity)
            w = jnp.exp2(s[e * CHUNK : (e + 1) * CHUNK])
            parts.append(jnp.where(row <= seen, w, 0.0).astype(BF16))
        weights = jnp.concatenate(parts, axis=0)
        acc[:, cols] += lax.dot_general(vt[:, part], weights, MATMUL, preferred_element_type=F32)
        return carry

    lax.fori_loop(0, rows // COLS, body, 0)


def add_block(step, other, place, block, q2, qpos, acc, kmax, k2, vt):
    zk = source(place, step, other)
    rows = block.shape[0]

    @pl.when(jnp.logical_or(zk <= owner(place, 0), zk <= owner(place, 1)))
    def _():
        load_keys(block[...], rows, k2, vt, kmax)

    for half in range(2):

        @pl.when(zk < owner(place, half))
        def _(half=half):
            all_before(rows, half, q2, k2, vt, acc)

        if (step == 0 and half == 0) or (step % 2 == 1 and half == 1):

            @pl.when(zk == owner(place, half))
            def _(half=half):
                first = 1 - place[2] if other else place[2]
                diagonal(place, rows, half, first, q2, qpos, k2, vt, acc)


def step_kernel(step, other, place, q2, qpos, block, acc_in, kmax_in, acc, kmax, k2, vt):
    acc[...] = acc_in[...]
    kmax[...] = kmax_in[...]
    add_block(step, other, place, block, q2, qpos, acc, kmax, k2, vt)


def first_kernel(place, q2, qpos, own, other, acc, kmax, k2, vt):
    acc[...] = jnp.zeros_like(acc)
    kmax[...] = jnp.zeros_like(kmax)
    add_block(0, False, place, own, q2, qpos, acc, kmax, k2, vt)
    add_block(0, True, place, other, q2, qpos, acc, kmax, k2, vt)


def in_range(q2, kmax):
    most = jnp.broadcast_to(jnp.max(kmax[...], axis=0, keepdims=True), (8, 128)).astype(BF16)
    bound = lax.dot_general(most, jnp.abs(q2[...]), MATMUL, preferred_element_type=F32)
    return jnp.max(bound) <= LIMIT


def slow_block(place, zk, first, block, q2, qpos, acc, top, held, k2, vt, kmax, sem):
    row = lax.broadcasted_iota(jnp.int32, (CHUNK, CHUNK), 0)

    def one(e, carry):
        copy = pltpu.make_async_copy(block.at[pl.ds(pl.multiple_of(e * CHUNK, CHUNK), CHUNK)], held, sem)
        copy.start()
        copy.wait()
        load_keys(held[...], CHUNK, k2, vt, kmax)
        parity = jnp.where(e < NX, first, 1 - first)

        def body(d, carry):
            ahead = NX * SPAN * (jnp.where(d < NX // 2, owner(place, 0), owner(place, 1)) - zk)
            base = SPAN * segment(place, lax.rem(e, NX)) + CHUNK * parity
            cols = pl.ds(pl.multiple_of(d * CHUNK, CHUNK), CHUNK)
            s = lax.dot_general(k2[:CHUNK, :], q2[:, cols], MATMUL, preferred_element_type=F32)
            keep = row <= qpos[:, cols] + (ahead - base)
            old = top[:1, cols]
            new = jnp.maximum(old, jnp.max(jnp.where(keep, s, -1e30), axis=0, keepdims=True))
            weights = jnp.where(keep, jnp.exp2(s - new), 0.0).astype(BF16)
            acc[:, cols] = acc[:, cols] * jnp.exp2(old - new) + lax.dot_general(
                vt[:, :CHUNK], weights, MATMUL, preferred_element_type=F32
            )
            top[:, cols] = jnp.broadcast_to(new, (8, CHUNK))
            return carry

        return lax.fori_loop(0, NX, body, carry)

    lax.fori_loop(0, block.shape[0] // CHUNK, one, 0)


def last_kernel(entries, place, q2, qpos, *refs):
    count = len(entries)
    block, kept = refs[0], refs[1 : 1 + count]
    acc_in, kmax_in, *outs = refs[1 + count : 3 + count + NX]
    acc, kmax, k2, vt, top, held, sem = refs[3 + count + NX :]
    acc[...] = acc_in[...]
    kmax[...] = kmax_in[...]
    add_block(*entries[-1], place, block, q2, qpos, acc, kmax, k2, vt)

    @pl.when(jnp.logical_not(in_range(q2, kmax)))
    def _():
        acc[...] = jnp.zeros_like(acc)
        top[...] = jnp.full(top.shape, -1e30, F32)
        for block, (step, other) in zip(kept, entries):
            first = 1 - place[2] if other else place[2]
            slow_block(place, source(place, step, other), first, block, q2, qpos, acc, top, held, k2, vt, kmax, sem)

    mixed = (acc[:HEAD_DIM, :] / acc[HEAD_DIM : HEAD_DIM + 1, :]).T
    mixed = mixed.reshape(2, NX, NY, ROWS, HEAD_DIM)
    for d in range(NX):
        both = jnp.concatenate([mixed[0, d], mixed[1, d]], axis=-1).astype(BF16)
        for y in range(NY):
            outs[d][pl.ds(lax.rem(y - place[3] + NY, NY), 1)] = both[y : y + 1]


def project_kernel(place, *refs):
    own, near, far, *outs = refs[NY:]
    lane = lax.broadcasted_iota(jnp.int32, (CHUNK // NY // 2, 128), 1) < HEAD_DIM
    even = place[2] == 0
    upper = lower = 0.0
    for e in range(NY):
        left, right = [], []
        for x in range(0, NX, 2):
            a = refs[e][pl.ds(lax.rem(x - place[1] + NX, NX), 1)][0].astype(F32)
            b = refs[e][pl.ds(lax.rem(x + 1 - place[1] + NX, NX), 1)][0].astype(F32)
            left.append(jnp.where(lane, a, pltpu.roll(b, HEAD_DIM, 1)))
            right.append(jnp.where(lane, pltpu.roll(a, HEAD_DIM, 1), b))
        if e == 0:
            w = own[...]
        else:
            left, right = ([jnp.where(even, *p), jnp.where(even, *p[::-1])] for p in (left, right))
            w = jnp.concatenate([near[(e - 1) * 128 : e * 128], far[(e - 1) * 128 : e * 128]], axis=0)
        upper += jnp.dot(jnp.concatenate(left, axis=1).astype(BF16), w, preferred_element_type=F32)
        lower += jnp.dot(jnp.concatenate(right, axis=1).astype(BF16), w, preferred_element_type=F32)
    outs[0][...] = upper.astype(BF16)
    outs[1][...] = lower.astype(BF16)


STATE = [jax.ShapeDtypeStruct((VROWS, COLS), F32), jax.ShapeDtypeStruct((8, 128), F32)]


def room(rows):
    return [pltpu.VMEM((rows, 128), BF16), pltpu.VMEM((VROWS, rows), BF16)]


def params():
    return pltpu.CompilerParams(vmem_limit_bytes=VMEM_LIMIT)


def cost(keys):
    return pl.CostEstimate(flops=keys, bytes_accessed=keys, transcendentals=0)


def split_heads(key_rows, value_rows, queries):
    return pl.pallas_call(
        split_kernel,
        in_specs=[in_hbm()] * 3,
        out_specs=[whole()] * (NX + 2),
        out_shape=[jax.ShapeDtypeStruct((CHUNK, 128), BF16)] * NX
        + [jax.ShapeDtypeStruct((CHUNK // 2, NX * HEAD_DIM), BF16)] * 2,
        scratch_shapes=[pltpu.VMEM((CHUNK, NX * HEAD_DIM), BF16)] * 3 + [pltpu.SemaphoreType.DMA((3,))],
        compiler_params=pltpu.CompilerParams(vmem_limit_bytes=60 << 20),
        name="split_heads",
    )(key_rows, value_rows, queries)


def pair_queries(place, here, there):
    return pl.pallas_call(
        pair_kernel,
        in_specs=[scalars(), whole(), whole()],
        out_specs=[whole()] * NX,
        out_shape=[jax.ShapeDtypeStruct((CHUNK // 2, 128), BF16)] * NX,
        compiler_params=params(),
        name="pair_queries",
    )(place, here, there)


def scale_queries(q):
    return pl.pallas_call(
        queries_kernel,
        out_shape=jax.ShapeDtypeStruct((128, COLS), BF16),
        compiler_params=params(),
        name="scale_queries",
    )(*q)


def first_step(place, q2, qpos, own, other):
    return pl.pallas_call(
        first_kernel,
        in_specs=[scalars()] + [whole()] * 4,
        out_specs=[whole(), whole()],
        out_shape=STATE,
        scratch_shapes=room(own.shape[0]),
        compiler_params=params(),
        cost_estimate=cost(COLS),
        name="own_block",
    )(place, q2, qpos, own, other)


def next_step(place, q2, qpos, block, state, step, other):
    return pl.pallas_call(
        functools.partial(step_kernel, step, other),
        in_specs=[scalars()] + [whole()] * 5,
        out_specs=[whole(), whole()],
        out_shape=STATE,
        input_output_aliases={4: 0, 5: 1},
        scratch_shapes=room(block.shape[0]),
        compiler_params=params(),
        cost_estimate=cost(COLS),
        name="block_%d_%d" % (step, other),
    )(place, q2, qpos, block, *state)


def last_step(place, q2, qpos, block, state, kept, entries):
    return pl.pallas_call(
        functools.partial(last_kernel, entries),
        in_specs=[scalars()] + [whole()] * 3 + [anywhere()] * len(kept) + [whole()] * 2,
        out_specs=[whole()] * NX,
        out_shape=[jax.ShapeDtypeStruct((NY, CHUNK // NY // 2, 128), BF16)] * NX,
        scratch_shapes=[
            pltpu.VMEM((VROWS, COLS), F32),
            pltpu.VMEM((8, 128), F32),
            *room(block.shape[0]),
            pltpu.VMEM((8, COLS), F32),
            pltpu.VMEM((CHUNK, 128), BF16),
            pltpu.SemaphoreType.DMA,
        ],
        compiler_params=params(),
        cost_estimate=cost(COLS),
        name="last_block",
    )(place, q2, qpos, block, *kept, *state)


def move(a, axis, size, by):
    return lax.ppermute(a, axis, [(i, (i + by) % size) for i in range(size)])


def move_ring(a):
    pairs = [(z * NC + c, (z + 1 - 2 * c) % NZ * NC + c) for z in range(NZ) for c in range(NC)]
    return lax.ppermute(a, ("z", "c"), pairs)


def mirror(a):
    return lax.ppermute(a, "z", [(z, NZ - 1 - z) for z in range(NZ)])


def query_positions(place):
    n = jnp.arange(COLS, dtype=jnp.int32).reshape(1, COLS)
    half, d, y, row = n // WIDE, n % WIDE // (NY * ROWS), n // ROWS % NY, n % ROWS
    return SPAN * ((place[1] - d + NX) % NX) + CHUNK * place[2] + ROWS * (2 * y + half) + row


def per_device(queries, key_rows, value_rows, out_weight):
    place = jnp.stack([lax.axis_index(a) for a in ("z", "x", "c", "y")]).astype(jnp.int32)
    *pieces, here, there = split_heads(key_rows, value_rows, queries)
    there = mirror(there)
    own = jnp.concatenate([pieces[0]] + [move(pieces[d], "x", NX, d) for d in range(1, NX)], axis=0)
    own, there, out_weight = lax.optimization_barrier((own, there, out_weight))
    other = move(own, "c", NC, 1)
    first = move_ring(own)
    q = pair_queries(place, here, there)
    q2 = scale_queries([q[0]] + [move(q[d], "x", NX, d) for d in range(1, NX)])
    qpos = query_positions(place)
    other, out_weight = lax.optimization_barrier((other, out_weight))
    half = out_weight.shape[0] // NC
    quarter = half // 2
    mine = lax.dynamic_slice_in_dim(out_weight, place[2] * half, half, 0)
    after, before = move(mine, "y", NY, 1), move(mine, "y", NY, -1)
    block = jnp.concatenate([first, move_ring(other)], axis=0)
    block, q2 = lax.optimization_barrier((block, q2))
    state = first_step(place, q2, qpos, own, other)
    kept, entries = [own, other], [(0, False), (0, True)]
    for t in range(1, NZ // 2):
        ahead = move_ring(block if t < NZ // 2 - 1 else block[:COLS])
        if t == 1:
            ahead, state, after, before = lax.optimization_barrier((ahead, state, after, before))
            across = [move(after[:quarter], "y", NY, 1), move(before[quarter:], "y", NY, -1)]
        elif t == 2:
            ahead, state, across = lax.optimization_barrier((ahead, state, across))
            near = jnp.concatenate([after, *across, before], axis=0)
            far = move(near, "c", NC, 1)
        else:
            ahead, state, near, far = lax.optimization_barrier((ahead, state, near, far))
        other = move(block, "c", NC, 1)
        kept += [block, other]
        entries += [(t, False), (t, True)]
        state = next_step(place, q2, qpos, block, state, t, False)
        state = next_step(place, q2, qpos, other, state, t, True)
        block = ahead
    t = NZ // 2
    other = move(block, "c", NC, 1)
    kept += [block, other]
    entries += [(t, False), (t, True)]
    state = next_step(place, q2, qpos, block, state, t, False)
    out = last_step(place, q2, qpos, other, state, kept, tuple(entries))
    out = [out[0]] + [move(out[d], "x", NX, -d) for d in range(1, NX)]
    out = [jnp.stack([out[d][e] for d in range(NX)]) for e in range(NY)]
    out = [out[0]] + [move(out[e], "y", NY, e) for e in range(1, NY)]
    here, there = pl.pallas_call(
        project_kernel,
        in_specs=[scalars()] + [whole()] * (NY + 3),
        out_specs=[whole()] * 2,
        out_shape=[jax.ShapeDtypeStruct((ROWS, 1024), BF16)] * 2,
        compiler_params=params(),
        name="project",
    )(place, *out, out_weight, near, far)
    return jnp.concatenate([here, mirror(there)], axis=0)


def solution(mesh):
    split = Mesh(mesh.devices.reshape(NZ, NX, NC, NY), ("z", "x", "c", "y"))
    rows = ("z", "x", "c")
    return jax.shard_map(
        per_device,
        mesh=split,
        in_specs=(P(rows, "y"), P(rows, "y"), P(rows, "y"), P("y", None)),
        out_specs=P((*rows, "y"), None),
        check_vma=False,
    )
```

```python
import functools
import math

import jax
import jax.numpy as jnp
from jax import lax
from jax.experimental import pallas as pl
from jax.experimental.pallas import tpu as pltpu
from jax.sharding import Mesh, PartitionSpec as P

HEAD_DIM = 64
F32 = jnp.float32
BF16 = jnp.bfloat16
MATMUL = (((1,), (0,)), ((), ()))

NZ, NX, NC, NY = 8, 4, 2, 4
CHUNK = 384
COLS = NX * CHUNK
SPAN = NC * CHUNK
WIDE = COLS // 2
ROWS = CHUNK // NY // 2
VROWS = 80
LIMIT = 90.0
VMEM_LIMIT = 40 << 20


def whole():
    return pl.BlockSpec(memory_space=pltpu.VMEM)


def scalars():
    return pl.BlockSpec(memory_space=pltpu.SMEM)


def anywhere():
    return pl.BlockSpec(memory_space=pl.ANY)


def in_hbm():
    return pl.BlockSpec(memory_space=pltpu.HBM)


def split_kernel(k_hbm, v_hbm, q_hbm, *refs):
    outs, (k_ref, v_ref, q_ref, sems) = refs[: NX + 2], refs[NX + 2 :]
    pairs = ((k_hbm, k_ref), (v_hbm, v_ref), (q_hbm, q_ref))
    copies = [pltpu.make_async_copy(src, dst, sems.at[i]) for i, (src, dst) in enumerate(pairs)]
    for copy in copies:
        copy.start()
    for copy in copies:
        copy.wait()
    shift = lax.rem(COLS - HEAD_DIM * lax.axis_index("x"), NX * HEAD_DIM)
    k, v = (pltpu.roll(r[...].astype(F32), shift, 1) for r in (k_ref, v_ref))
    for d in range(NX):
        cols = slice(d * HEAD_DIM, (d + 1) * HEAD_DIM)
        outs[d][...] = jnp.concatenate([k[:, cols], v[:, cols]], axis=1).astype(BF16)
    for y in range(NY):
        for half in range(2):
            outs[NX + half][y * ROWS : (y + 1) * ROWS, :] = q_ref[pl.ds((2 * y + half) * ROWS, ROWS), :]


def pair_kernel(place, a_ref, b_ref, *outs):
    shift = lax.rem(COLS - HEAD_DIM * place[1], NX * HEAD_DIM)
    a, b = (pltpu.roll(r[...].astype(F32), shift, 1) for r in (a_ref, b_ref))
    for d in range(NX):
        cols = slice(d * HEAD_DIM, (d + 1) * HEAD_DIM)
        outs[d][...] = jnp.concatenate([a[:, cols], b[:, cols]], axis=1).astype(BF16)


def queries_kernel(*refs):
    for half in range(2):
        cols = slice(half * HEAD_DIM, (half + 1) * HEAD_DIM)
        q = jnp.concatenate([refs[d][...].astype(F32)[:, cols] for d in range(NX)], axis=0)
        q = q * (math.log2(math.e) / math.sqrt(HEAD_DIM))
        high = q.astype(BF16).astype(F32)
        both = jnp.concatenate([high, q - high], axis=1)
        refs[NX][:, half * WIDE : (half + 1) * WIDE] = both.T.astype(BF16)


def load_keys(kv, rows, k2, vt, kmax):
    keys, values = kv[:, :HEAD_DIM], kv[:, HEAD_DIM:]
    twice = jnp.concatenate([keys, keys], axis=1)
    k2[:rows, :] = twice
    vt[:HEAD_DIM, :rows] = values.T
    vt[HEAD_DIM:, :rows] = jnp.ones((VROWS - HEAD_DIM, rows), BF16)
    largest = jnp.max(jnp.abs(twice.astype(F32)).reshape(rows // 8, 8, 128), axis=0)
    kmax[...] = jnp.maximum(kmax[...], largest)


def segment(place, d):
    return lax.rem(place[1] - d + NX, NX)


def owner(place, half):
    return place[0] if half == 0 else NZ - 1 - place[0]


def source(place, step, other):
    ahead = (place[2] == 1) != other
    return lax.rem(place[0] + jnp.where(ahead, step, NZ - step), NZ)


def all_before(rows, half, q2, k2, vt, acc):
    cols = slice(half * WIDE, (half + 1) * WIDE)

    qb = q2[:, cols]
    total = acc[:, cols]
    for start in range(0, rows, WIDE):
        part = slice(start, start + WIDE)
        s = lax.dot_general(k2[part, :], qb, MATMUL, preferred_element_type=F32)
        weights = jnp.exp2(s).astype(BF16)
        total = total + lax.dot_general(vt[:, part], weights, MATMUL, preferred_element_type=F32)
    acc[:, cols] = total


def diagonal(place, rows, half, first, q2, qpos, k2, vt, acc):
    cols = slice(half * WIDE, (half + 1) * WIDE)
    row = lax.broadcasted_iota(jnp.int32, (CHUNK, WIDE), 0)

    def body(i, carry):
        parity = jnp.where(i == 0, first, 1 - first)
        part = pl.ds(pl.multiple_of(i * COLS, COLS), COLS)
        s = lax.dot_general(k2[part, :], q2[:, cols], MATMUL, preferred_element_type=F32)
        parts = []
        for e in range(NX):
            seen = qpos[:, cols] - (SPAN * segment(place, e) + CHUNK * parity)
            w = jnp.exp2(s[e * CHUNK : (e + 1) * CHUNK])
            parts.append(jnp.where(row <= seen, w, 0.0).astype(BF16))
        weights = jnp.concatenate(parts, axis=0)
        acc[:, cols] += lax.dot_general(vt[:, part], weights, MATMUL, preferred_element_type=F32)
        return carry

    lax.fori_loop(0, rows // COLS, body, 0)


def add_block(step, other, place, block, q2, qpos, acc, kmax, k2, vt):
    zk = source(place, step, other)
    rows = block.shape[0]

    @pl.when(jnp.logical_or(zk <= owner(place, 0), zk <= owner(place, 1)))
    def _():
        load_keys(block[...], rows, k2, vt, kmax)

    for half in range(2):

        @pl.when(zk < owner(place, half))
        def _(half=half):
            all_before(rows, half, q2, k2, vt, acc)

        if (step == 0 and half == 0) or (step % 2 == 1 and half == 1):

            @pl.when(zk == owner(place, half))
            def _(half=half):
                first = 1 - place[2] if other else place[2]
                diagonal(place, rows, half, first, q2, qpos, k2, vt, acc)


def step_kernel(step, other, place, q2, qpos, block, acc_in, kmax_in, acc, kmax, k2, vt):
    acc[...] = acc_in[...]
    kmax[...] = kmax_in[...]
    add_block(step, other, place, block, q2, qpos, acc, kmax, k2, vt)


def first_kernel(place, q2, qpos, own, other, acc, kmax, k2, vt):
    acc[...] = jnp.zeros_like(acc)
    kmax[...] = jnp.zeros_like(kmax)
    add_block(0, False, place, own, q2, qpos, acc, kmax, k2, vt)
    add_block(0, True, place, other, q2, qpos, acc, kmax, k2, vt)


def in_range(q2, kmax):
    most = jnp.broadcast_to(jnp.max(kmax[...], axis=0, keepdims=True), (8, 128)).astype(BF16)
    bound = lax.dot_general(most, jnp.abs(q2[...]), MATMUL, preferred_element_type=F32)
    return jnp.max(bound) <= LIMIT


def slow_blocks(place, kept, entries, q2, qpos, acc, top, held, k2, vt, kmax, sem):
    row = lax.broadcasted_iota(jnp.int32, (CHUNK, CHUNK), 0)

    def one(i, carry):
        n, e = i // (NC * NX), lax.rem(i, NC * NX)
        step = first = count = 0
        for m, (block, (its_step, other)) in enumerate(zip(kept, entries)):
            here = n == m
            size = block.shape[0] // CHUNK
            step = jnp.where(here, its_step, step)
            first = jnp.where(here, 1 - place[2] if other else place[2], first)
            count = jnp.where(here, size, count)

            @pl.when(jnp.logical_and(here, e < size))
            def _(block=block):
                part = pl.ds(pl.multiple_of(e * CHUNK, CHUNK), CHUNK)
                copy = pltpu.make_async_copy(block.at[part], held, sem)
                copy.start()
                copy.wait()

        zk = lax.rem(place[0] + jnp.where(first == 1, step, NZ - step), NZ)
        parity = jnp.where(e < NX, first, 1 - first)

        @pl.when(e < count)
        def _():
            load_keys(held[...], CHUNK, k2, vt, kmax)

            def body(d, carry):
                ahead = NX * SPAN * (jnp.where(d < NX // 2, owner(place, 0), owner(place, 1)) - zk)
                base = SPAN * segment(place, lax.rem(e, NX)) + CHUNK * parity
                cols = pl.ds(pl.multiple_of(d * CHUNK, CHUNK), CHUNK)
                s = lax.dot_general(k2[:CHUNK, :], q2[:, cols], MATMUL, preferred_element_type=F32)
                keep = row <= qpos[:, cols] + (ahead - base)
                old = top[:1, cols]
                new = jnp.maximum(old, jnp.max(jnp.where(keep, s, -1e30), axis=0, keepdims=True))
                weights = jnp.where(keep, jnp.exp2(s - new), 0.0).astype(BF16)
                acc[:, cols] = acc[:, cols] * jnp.exp2(old - new) + lax.dot_general(
                    vt[:, :CHUNK], weights, MATMUL, preferred_element_type=F32
                )
                top[:, cols] = jnp.broadcast_to(new, (8, CHUNK))
                return carry

            lax.fori_loop(0, NX, body, 0)

        return carry

    lax.fori_loop(0, len(entries) * NC * NX, one, 0)


def last_kernel(entries, place, q2, qpos, *refs):
    count = len(entries)
    block, kept = refs[0], refs[1 : 1 + count]
    acc_in, kmax_in, *outs = refs[1 + count : 3 + count + NX]
    acc, kmax, k2, vt, top, held, sem = refs[3 + count + NX :]
    acc[...] = acc_in[...]
    kmax[...] = kmax_in[...]
    add_block(*entries[-1], place, block, q2, qpos, acc, kmax, k2, vt)

    @pl.when(jnp.logical_not(in_range(q2, kmax)))
    def _():
        acc[...] = jnp.zeros_like(acc)
        top[...] = jnp.full(top.shape, -1e30, F32)
        slow_blocks(place, kept, entries, q2, qpos, acc, top, held, k2, vt, kmax, sem)

    mixed = (acc[:HEAD_DIM, :] / acc[HEAD_DIM : HEAD_DIM + 1, :]).T
    mixed = mixed.reshape(2, NX, NY, ROWS, HEAD_DIM)
    for d in range(NX):
        both = jnp.concatenate([mixed[0, d], mixed[1, d]], axis=-1).astype(BF16)
        for y in range(NY):
            outs[d][pl.ds(lax.rem(y - place[3] + NY, NY), 1)] = both[y : y + 1]


def project_kernel(place, *refs):
    own, near, far, *outs = refs[NY:]
    lane = lax.broadcasted_iota(jnp.int32, (CHUNK // NY // 2, 128), 1) < HEAD_DIM
    even = place[2] == 0
    upper = lower = 0.0
    for e in range(NY):
        left, right = [], []
        for x in range(0, NX, 2):
            a = refs[e][pl.ds(lax.rem(x - place[1] + NX, NX), 1)][0].astype(F32)
            b = refs[e][pl.ds(lax.rem(x + 1 - place[1] + NX, NX), 1)][0].astype(F32)
            left.append(jnp.where(lane, a, pltpu.roll(b, HEAD_DIM, 1)))
            right.append(jnp.where(lane, pltpu.roll(a, HEAD_DIM, 1), b))
        if e == 0:
            w = own[...]
        else:
            left, right = ([jnp.where(even, *p), jnp.where(even, *p[::-1])] for p in (left, right))
            w = jnp.concatenate([near[(e - 1) * 128 : e * 128], far[(e - 1) * 128 : e * 128]], axis=0)
        upper += jnp.dot(jnp.concatenate(left, axis=1).astype(BF16), w, preferred_element_type=F32)
        lower += jnp.dot(jnp.concatenate(right, axis=1).astype(BF16), w, preferred_element_type=F32)
    outs[0][...] = upper.astype(BF16)
    outs[1][...] = lower.astype(BF16)


STATE = [jax.ShapeDtypeStruct((VROWS, COLS), F32), jax.ShapeDtypeStruct((8, 128), F32)]


def room(rows):
    return [pltpu.VMEM((rows, 128), BF16), pltpu.VMEM((VROWS, rows), BF16)]


def params():
    return pltpu.CompilerParams(vmem_limit_bytes=VMEM_LIMIT)


def cost(keys):
    return pl.CostEstimate(flops=keys, bytes_accessed=keys, transcendentals=0)


def split_heads(key_rows, value_rows, queries):
    return pl.pallas_call(
        split_kernel,
        in_specs=[in_hbm()] * 3,
        out_specs=[whole()] * (NX + 2),
        out_shape=[jax.ShapeDtypeStruct((CHUNK, 128), BF16)] * NX
        + [jax.ShapeDtypeStruct((CHUNK // 2, NX * HEAD_DIM), BF16)] * 2,
        scratch_shapes=[pltpu.VMEM((CHUNK, NX * HEAD_DIM), BF16)] * 3 + [pltpu.SemaphoreType.DMA((3,))],
        compiler_params=pltpu.CompilerParams(vmem_limit_bytes=60 << 20),
        name="split_heads",
    )(key_rows, value_rows, queries)


def pair_queries(place, here, there):
    return pl.pallas_call(
        pair_kernel,
        in_specs=[scalars(), whole(), whole()],
        out_specs=[whole()] * NX,
        out_shape=[jax.ShapeDtypeStruct((CHUNK // 2, 128), BF16)] * NX,
        compiler_params=params(),
        name="pair_queries",
    )(place, here, there)


def scale_queries(q):
    return pl.pallas_call(
        queries_kernel,
        out_shape=jax.ShapeDtypeStruct((128, COLS), BF16),
        compiler_params=params(),
        name="scale_queries",
    )(*q)


def first_step(place, q2, qpos, own, other):
    return pl.pallas_call(
        first_kernel,
        in_specs=[scalars()] + [whole()] * 4,
        out_specs=[whole(), whole()],
        out_shape=STATE,
        scratch_shapes=room(own.shape[0]),
        compiler_params=params(),
        cost_estimate=cost(COLS),
        name="own_block",
    )(place, q2, qpos, own, other)


def next_step(place, q2, qpos, block, state, step, other):
    return pl.pallas_call(
        functools.partial(step_kernel, step, other),
        in_specs=[scalars()] + [whole()] * 5,
        out_specs=[whole(), whole()],
        out_shape=STATE,
        input_output_aliases={4: 0, 5: 1},
        scratch_shapes=room(block.shape[0]),
        compiler_params=params(),
        cost_estimate=cost(COLS),
        name="block_%d_%d" % (step, other),
    )(place, q2, qpos, block, *state)


def last_step(place, q2, qpos, block, state, kept, entries):
    return pl.pallas_call(
        functools.partial(last_kernel, entries),
        in_specs=[scalars()] + [whole()] * 3 + [anywhere()] * len(kept) + [whole()] * 2,
        out_specs=[whole()] * NX,
        out_shape=[jax.ShapeDtypeStruct((NY, CHUNK // NY // 2, 128), BF16)] * NX,
        scratch_shapes=[
            pltpu.VMEM((VROWS, COLS), F32),
            pltpu.VMEM((8, 128), F32),
            *room(block.shape[0]),
            pltpu.VMEM((8, COLS), F32),
            pltpu.VMEM((CHUNK, 128), BF16),
            pltpu.SemaphoreType.DMA,
        ],
        compiler_params=params(),
        cost_estimate=cost(COLS),
        name="last_block",
    )(place, q2, qpos, block, *kept, *state)


def move(a, axis, size, by):
    return lax.ppermute(a, axis, [(i, (i + by) % size) for i in range(size)])


def move_ring(a):
    pairs = [(z * NC + c, (z + 1 - 2 * c) % NZ * NC + c) for z in range(NZ) for c in range(NC)]
    return lax.ppermute(a, ("z", "c"), pairs)


def mirror(a):
    return lax.ppermute(a, "z", [(z, NZ - 1 - z) for z in range(NZ)])


def query_positions(place):
    n = jnp.arange(COLS, dtype=jnp.int32).reshape(1, COLS)
    half, d, y, row = n // WIDE, n % WIDE // (NY * ROWS), n // ROWS % NY, n % ROWS
    return SPAN * ((place[1] - d + NX) % NX) + CHUNK * place[2] + ROWS * (2 * y + half) + row


def per_device(queries, key_rows, value_rows, out_weight):
    place = jnp.stack([lax.axis_index(a) for a in ("z", "x", "c", "y")]).astype(jnp.int32)
    *pieces, here, there = split_heads(key_rows, value_rows, queries)
    there = mirror(there)
    own = jnp.concatenate([pieces[0]] + [move(pieces[d], "x", NX, d) for d in range(1, NX)], axis=0)
    own, there, out_weight = lax.optimization_barrier((own, there, out_weight))
    other = move(own, "c", NC, 1)
    first = move_ring(own)
    q = pair_queries(place, here, there)
    q2 = scale_queries([q[0]] + [move(q[d], "x", NX, d) for d in range(1, NX)])
    qpos = query_positions(place)
    other, out_weight = lax.optimization_barrier((other, out_weight))
    half = out_weight.shape[0] // NC
    mine = lax.dynamic_slice_in_dim(out_weight, place[2] * half, half, 0)
    after, before = move(mine, "y", NY, 1), move(mine, "y", NY, -1)
    block = jnp.concatenate([first, move_ring(other)], axis=0)
    block, q2 = lax.optimization_barrier((block, q2))
    state = first_step(place, q2, qpos, own, other)
    kept, entries = [own, other], [(0, False), (0, True)]
    for t in range(1, NZ // 2):
        ahead = move_ring(block if t < NZ // 2 - 1 else block[:COLS])
        if t == 1:
            ahead, state, after, before = lax.optimization_barrier((ahead, state, after, before))
            across = move(after, "y", NY, 1)
        elif t == 2:
            ahead, state, across = lax.optimization_barrier((ahead, state, across))
            near = jnp.concatenate([after, across, before], axis=0)
            far = move(near, "c", NC, 1)
        else:
            ahead, state, near, far = lax.optimization_barrier((ahead, state, near, far))
        other = move(block, "c", NC, 1)
        kept += [block, other]
        entries += [(t, False), (t, True)]
        state = next_step(place, q2, qpos, block, state, t, False)
        state = next_step(place, q2, qpos, other, state, t, True)
        block = ahead
    t = NZ // 2
    other = move(block, "c", NC, 1)
    kept += [block, other]
    entries += [(t, False), (t, True)]
    state = next_step(place, q2, qpos, block, state, t, False)
    out = last_step(place, q2, qpos, other, state, kept, tuple(entries))
    out = [out[0]] + [move(out[d], "x", NX, -d) for d in range(1, NX)]
    out = [jnp.stack([out[d][e] for d in range(NX)]) for e in range(NY)]
    out = [out[0]] + [move(out[e], "y", NY, e) for e in range(1, NY)]
    here, there = pl.pallas_call(
        project_kernel,
        in_specs=[scalars()] + [whole()] * (NY + 3),
        out_specs=[whole()] * 2,
        out_shape=[jax.ShapeDtypeStruct((ROWS, 1024), BF16)] * 2,
        compiler_params=params(),
        name="project",
    )(place, *out, out_weight, near, far)
    return jnp.concatenate([here, mirror(there)], axis=0)


def solution(mesh):
    split = Mesh(mesh.devices.reshape(NZ, NX, NC, NY), ("z", "x", "c", "y"))
    rows = ("z", "x", "c")
    return jax.shard_map(
        per_device,
        mesh=split,
        in_specs=(P(rows, "y"), P(rows, "y"), P(rows, "y"), P("y", None)),
        out_specs=P((*rows, "y"), None),
        check_vma=False,
    )
```

```python
import functools
import math

import jax
import jax.numpy as jnp
from jax import lax
from jax.experimental import pallas as pl
from jax.experimental.pallas import tpu as pltpu
from jax.sharding import Mesh, PartitionSpec as P

HEAD_DIM = 64
F32 = jnp.float32
BF16 = jnp.bfloat16
MATMUL = (((1,), (0,)), ((), ()))

NZ, NX, NC, NY = 8, 4, 2, 4
CHUNK = 384
COLS = NX * CHUNK
SPAN = NC * CHUNK
WIDE = COLS // 2
ROWS = CHUNK // NY // 2
VROWS = 80
LIMIT = 90.0
VMEM_LIMIT = 40 << 20


def whole():
    return pl.BlockSpec(memory_space=pltpu.VMEM)


def scalars():
    return pl.BlockSpec(memory_space=pltpu.SMEM)


def anywhere():
    return pl.BlockSpec(memory_space=pl.ANY)


def in_hbm():
    return pl.BlockSpec(memory_space=pltpu.HBM)


def split_kernel(k_hbm, v_hbm, q_hbm, *refs):
    outs, (k_ref, v_ref, q_ref, sems) = refs[: NX + 2], refs[NX + 2 :]
    pairs = ((k_hbm, k_ref), (v_hbm, v_ref), (q_hbm, q_ref))
    copies = [pltpu.make_async_copy(src, dst, sems.at[i]) for i, (src, dst) in enumerate(pairs)]
    for copy in copies:
        copy.start()
    for copy in copies:
        copy.wait()
    shift = lax.rem(COLS - HEAD_DIM * lax.axis_index("x"), NX * HEAD_DIM)
    k, v = (pltpu.roll(r[...].astype(F32), shift, 1) for r in (k_ref, v_ref))
    for d in range(NX):
        cols = slice(d * HEAD_DIM, (d + 1) * HEAD_DIM)
        outs[d][...] = jnp.concatenate([k[:, cols], v[:, cols]], axis=1).astype(BF16)
    for y in range(NY):
        for half in range(2):
            outs[NX + half][y * ROWS : (y + 1) * ROWS, :] = q_ref[pl.ds((2 * y + half) * ROWS, ROWS), :]


def pair_kernel(place, a_ref, b_ref, *outs):
    shift = lax.rem(COLS - HEAD_DIM * place[1], NX * HEAD_DIM)
    a, b = (pltpu.roll(r[...].astype(F32), shift, 1) for r in (a_ref, b_ref))
    for d in range(NX):
        cols = slice(d * HEAD_DIM, (d + 1) * HEAD_DIM)
        outs[d][...] = jnp.concatenate([a[:, cols], b[:, cols]], axis=1).astype(BF16)


def queries_kernel(*refs):
    for half in range(2):
        cols = slice(half * HEAD_DIM, (half + 1) * HEAD_DIM)
        q = jnp.concatenate([refs[d][...].astype(F32)[:, cols] for d in range(NX)], axis=0)
        q = q * (math.log2(math.e) / math.sqrt(HEAD_DIM))
        high = q.astype(BF16).astype(F32)
        both = jnp.concatenate([high, q - high], axis=1)
        refs[NX][:, half * WIDE : (half + 1) * WIDE] = both.T.astype(BF16)


def load_keys(kv, rows, k2, vt, kmax):
    keys, values = kv[:, :HEAD_DIM], kv[:, HEAD_DIM:]
    twice = jnp.concatenate([keys, keys], axis=1)
    k2[:rows, :] = twice
    vt[:HEAD_DIM, :rows] = values.T
    vt[HEAD_DIM:, :rows] = jnp.ones((VROWS - HEAD_DIM, rows), BF16)
    largest = jnp.max(jnp.abs(twice.astype(F32)).reshape(rows // 8, 8, 128), axis=0)
    kmax[...] = jnp.maximum(kmax[...], largest)


def segment(place, d):
    return lax.rem(place[1] - d + NX, NX)


def owner(place, half):
    return place[0] if half == 0 else NZ - 1 - place[0]


def source(place, step, other):
    ahead = (place[2] == 1) != other
    return lax.rem(place[0] + jnp.where(ahead, step, NZ - step), NZ)


def all_before(rows, half, q2, k2, vt, acc):
    cols = slice(half * WIDE, (half + 1) * WIDE)

    qb = q2[:, cols]
    total = acc[:, cols]
    for start in range(0, rows, WIDE):
        part = slice(start, start + WIDE)
        s = lax.dot_general(k2[part, :], qb, MATMUL, preferred_element_type=F32)
        weights = jnp.exp2(s).astype(BF16)
        total = total + lax.dot_general(vt[:, part], weights, MATMUL, preferred_element_type=F32)
    acc[:, cols] = total


def diagonal(place, rows, half, first, q2, qpos, k2, vt, acc):
    cols = slice(half * WIDE, (half + 1) * WIDE)
    row = lax.broadcasted_iota(jnp.int32, (CHUNK, WIDE), 0)

    def body(i, carry):
        parity = jnp.where(i == 0, first, 1 - first)
        part = pl.ds(pl.multiple_of(i * COLS, COLS), COLS)
        s = lax.dot_general(k2[part, :], q2[:, cols], MATMUL, preferred_element_type=F32)
        parts = []
        for e in range(NX):
            seen = qpos[:, cols] - (SPAN * segment(place, e) + CHUNK * parity)
            w = jnp.exp2(s[e * CHUNK : (e + 1) * CHUNK])
            parts.append(jnp.where(row <= seen, w, 0.0).astype(BF16))
        weights = jnp.concatenate(parts, axis=0)
        acc[:, cols] += lax.dot_general(vt[:, part], weights, MATMUL, preferred_element_type=F32)
        return carry

    lax.fori_loop(0, rows // COLS, body, 0)


def add_block(step, other, place, block, q2, qpos, acc, kmax, k2, vt):
    zk = source(place, step, other)
    rows = block.shape[0]

    @pl.when(jnp.logical_or(zk <= owner(place, 0), zk <= owner(place, 1)))
    def _():
        load_keys(block[...], rows, k2, vt, kmax)

    for half in range(2):

        @pl.when(zk < owner(place, half))
        def _(half=half):
            all_before(rows, half, q2, k2, vt, acc)

        if (step == 0 and half == 0) or (step % 2 == 1 and half == 1):

            @pl.when(zk == owner(place, half))
            def _(half=half):
                first = 1 - place[2] if other else place[2]
                diagonal(place, rows, half, first, q2, qpos, k2, vt, acc)


def step_kernel(step, other, place, q2, qpos, block, acc_in, kmax_in, acc, kmax, k2, vt):
    acc[...] = acc_in[...]
    kmax[...] = kmax_in[...]
    add_block(step, other, place, block, q2, qpos, acc, kmax, k2, vt)


def first_kernel(place, q2, qpos, own, other, acc, kmax, k2, vt):
    acc[...] = jnp.zeros_like(acc)
    kmax[...] = jnp.zeros_like(kmax)
    add_block(0, False, place, own, q2, qpos, acc, kmax, k2, vt)
    add_block(0, True, place, other, q2, qpos, acc, kmax, k2, vt)


def in_range(q2, kmax):
    most = jnp.broadcast_to(jnp.max(kmax[...], axis=0, keepdims=True), (8, 128)).astype(BF16)
    bound = lax.dot_general(most, jnp.abs(q2[...]), MATMUL, preferred_element_type=F32)
    return jnp.max(bound) <= LIMIT


def slow_blocks(place, kept, entries, q2, qpos, acc, top, held, k2, vt, kmax, sem):
    row = lax.broadcasted_iota(jnp.int32, (CHUNK, CHUNK), 0)

    def one(i, carry):
        n, e = i // (NC * NX), lax.rem(i, NC * NX)
        step = first = count = 0
        for m, (block, (its_step, other)) in enumerate(zip(kept, entries)):
            here = n == m
            size = block.shape[0] // CHUNK
            step = jnp.where(here, its_step, step)
            first = jnp.where(here, 1 - place[2] if other else place[2], first)
            count = jnp.where(here, size, count)

            @pl.when(jnp.logical_and(here, e < size))
            def _(block=block):
                part = pl.ds(pl.multiple_of(e * CHUNK, CHUNK), CHUNK)
                copy = pltpu.make_async_copy(block.at[part], held, sem)
                copy.start()
                copy.wait()

        zk = lax.rem(place[0] + jnp.where(first == 1, step, NZ - step), NZ)
        parity = jnp.where(e < NX, first, 1 - first)

        @pl.when(e < count)
        def _():
            load_keys(held[...], CHUNK, k2, vt, kmax)

            def body(d, carry):
                ahead = NX * SPAN * (jnp.where(d < NX // 2, owner(place, 0), owner(place, 1)) - zk)
                base = SPAN * segment(place, lax.rem(e, NX)) + CHUNK * parity
                cols = pl.ds(pl.multiple_of(d * CHUNK, CHUNK), CHUNK)
                s = lax.dot_general(k2[:CHUNK, :], q2[:, cols], MATMUL, preferred_element_type=F32)
                keep = row <= qpos[:, cols] + (ahead - base)
                old = top[:1, cols]
                new = jnp.maximum(old, jnp.max(jnp.where(keep, s, -1e30), axis=0, keepdims=True))
                weights = jnp.where(keep, jnp.exp2(s - new), 0.0).astype(BF16)
                acc[:, cols] = acc[:, cols] * jnp.exp2(old - new) + lax.dot_general(
                    vt[:, :CHUNK], weights, MATMUL, preferred_element_type=F32
                )
                top[:, cols] = jnp.broadcast_to(new, (8, CHUNK))
                return carry

            lax.fori_loop(0, NX, body, 0)

        return carry

    lax.fori_loop(0, len(entries) * NC * NX, one, 0)


def last_kernel(entries, place, q2, qpos, *refs):
    count = len(entries)
    block, kept = refs[0], refs[1 : 1 + count]
    acc_in, kmax_in, *outs = refs[1 + count : 3 + count + NX]
    acc, kmax, k2, vt, top, held, sem = refs[3 + count + NX :]
    acc[...] = acc_in[...]
    kmax[...] = kmax_in[...]
    add_block(*entries[-1], place, block, q2, qpos, acc, kmax, k2, vt)

    @pl.when(jnp.logical_not(in_range(q2, kmax)))
    def _():
        acc[...] = jnp.zeros_like(acc)
        top[...] = jnp.full(top.shape, -1e30, F32)
        slow_blocks(place, kept, entries, q2, qpos, acc, top, held, k2, vt, kmax, sem)

    mixed = (acc[:HEAD_DIM, :] / acc[HEAD_DIM : HEAD_DIM + 1, :]).T
    mixed = mixed.reshape(2, NX, NY, ROWS, HEAD_DIM)
    for d in range(NX):
        both = jnp.concatenate([mixed[0, d], mixed[1, d]], axis=-1).astype(BF16)
        for y in range(NY):
            outs[d][pl.ds(lax.rem(y - place[3] + NY, NY), 1)] = both[y : y + 1]


def project_kernel(place, *refs):
    own, near, far, *outs = refs[NY:]
    lane = lax.broadcasted_iota(jnp.int32, (CHUNK // NY // 2, 128), 1) < HEAD_DIM
    even = place[2] == 0
    upper = lower = 0.0
    for e in range(NY):
        left, right = [], []
        for x in range(0, NX, 2):
            a = refs[e][pl.ds(lax.rem(x - place[1] + NX, NX), 1)][0].astype(F32)
            b = refs[e][pl.ds(lax.rem(x + 1 - place[1] + NX, NX), 1)][0].astype(F32)
            left.append(jnp.where(lane, a, pltpu.roll(b, HEAD_DIM, 1)))
            right.append(jnp.where(lane, pltpu.roll(a, HEAD_DIM, 1), b))
        if e == 0:
            w = own[...]
        else:
            left, right = ([jnp.where(even, *p), jnp.where(even, *p[::-1])] for p in (left, right))
            w = jnp.concatenate([near[(e - 1) * 128 : e * 128], far[(e - 1) * 128 : e * 128]], axis=0)
        upper += jnp.dot(jnp.concatenate(left, axis=1).astype(BF16), w, preferred_element_type=F32)
        lower += jnp.dot(jnp.concatenate(right, axis=1).astype(BF16), w, preferred_element_type=F32)
    outs[0][...] = upper.astype(BF16)
    outs[1][...] = lower.astype(BF16)


STATE = [jax.ShapeDtypeStruct((VROWS, COLS), F32), jax.ShapeDtypeStruct((8, 128), F32)]


def room(rows):
    return [pltpu.VMEM((rows, 128), BF16), pltpu.VMEM((VROWS, rows), BF16)]


def params():
    return pltpu.CompilerParams(vmem_limit_bytes=VMEM_LIMIT)


def cost(keys):
    return pl.CostEstimate(flops=keys, bytes_accessed=keys, transcendentals=0)


def split_heads(key_rows, value_rows, queries):
    return pl.pallas_call(
        split_kernel,
        in_specs=[in_hbm()] * 3,
        out_specs=[whole()] * (NX + 2),
        out_shape=[jax.ShapeDtypeStruct((CHUNK, 128), BF16)] * NX
        + [jax.ShapeDtypeStruct((CHUNK // 2, NX * HEAD_DIM), BF16)] * 2,
        scratch_shapes=[pltpu.VMEM((CHUNK, NX * HEAD_DIM), BF16)] * 3 + [pltpu.SemaphoreType.DMA((3,))],
        compiler_params=pltpu.CompilerParams(vmem_limit_bytes=60 << 20),
        name="split_heads",
    )(key_rows, value_rows, queries)


def pair_queries(place, here, there):
    return pl.pallas_call(
        pair_kernel,
        in_specs=[scalars(), whole(), whole()],
        out_specs=[whole()] * NX,
        out_shape=[jax.ShapeDtypeStruct((CHUNK // 2, 128), BF16)] * NX,
        compiler_params=params(),
        name="pair_queries",
    )(place, here, there)


def scale_queries(q):
    return pl.pallas_call(
        queries_kernel,
        out_shape=jax.ShapeDtypeStruct((128, COLS), BF16),
        compiler_params=params(),
        name="scale_queries",
    )(*q)


def first_step(place, q2, qpos, own, other):
    return pl.pallas_call(
        first_kernel,
        in_specs=[scalars()] + [whole()] * 4,
        out_specs=[whole(), whole()],
        out_shape=STATE,
        scratch_shapes=room(own.shape[0]),
        compiler_params=params(),
        cost_estimate=cost(COLS),
        name="own_block",
    )(place, q2, qpos, own, other)


def next_step(place, q2, qpos, block, state, step, other):
    return pl.pallas_call(
        functools.partial(step_kernel, step, other),
        in_specs=[scalars()] + [whole()] * 5,
        out_specs=[whole(), whole()],
        out_shape=STATE,
        input_output_aliases={4: 0, 5: 1},
        scratch_shapes=room(block.shape[0]),
        compiler_params=params(),
        cost_estimate=cost(COLS),
        name="block_%d_%d" % (step, other),
    )(place, q2, qpos, block, *state)


def last_step(place, q2, qpos, block, state, kept, entries):
    return pl.pallas_call(
        functools.partial(last_kernel, entries),
        in_specs=[scalars()] + [whole()] * 3 + [anywhere()] * len(kept) + [whole()] * 2,
        out_specs=[whole()] * NX,
        out_shape=[jax.ShapeDtypeStruct((NY, CHUNK // NY // 2, 128), BF16)] * NX,
        scratch_shapes=[
            pltpu.VMEM((VROWS, COLS), F32),
            pltpu.VMEM((8, 128), F32),
            *room(block.shape[0]),
            pltpu.VMEM((8, COLS), F32),
            pltpu.VMEM((CHUNK, 128), BF16),
            pltpu.SemaphoreType.DMA,
        ],
        compiler_params=params(),
        cost_estimate=cost(COLS),
        name="last_block",
    )(place, q2, qpos, block, *kept, *state)


def move(a, axis, size, by):
    return lax.ppermute(a, axis, [(i, (i + by) % size) for i in range(size)])


def move_ring(a):
    pairs = [(z * NC + c, (z + 1 - 2 * c) % NZ * NC + c) for z in range(NZ) for c in range(NC)]
    return lax.ppermute(a, ("z", "c"), pairs)


def mirror(a):
    return lax.ppermute(a, "z", [(z, NZ - 1 - z) for z in range(NZ)])


def query_positions(place):
    n = jnp.arange(COLS, dtype=jnp.int32).reshape(1, COLS)
    half, d, y, row = n // WIDE, n % WIDE // (NY * ROWS), n // ROWS % NY, n % ROWS
    return SPAN * ((place[1] - d + NX) % NX) + CHUNK * place[2] + ROWS * (2 * y + half) + row


def per_device(queries, key_rows, value_rows, out_weight):
    place = jnp.stack([lax.axis_index(a) for a in ("z", "x", "c", "y")]).astype(jnp.int32)
    *pieces, here, there = split_heads(key_rows, value_rows, queries)
    there = mirror(there)
    own = jnp.concatenate([pieces[0]] + [move(pieces[d], "x", NX, d) for d in range(1, NX)], axis=0)
    own, there, out_weight = lax.optimization_barrier((own, there, out_weight))
    other = move(own, "c", NC, 1)
    first = move_ring(own)
    q = pair_queries(place, here, there)
    q2 = scale_queries([q[0]] + [move(q[d], "x", NX, d) for d in range(1, NX)])
    qpos = query_positions(place)
    other, out_weight = lax.optimization_barrier((other, out_weight))
    half = out_weight.shape[0] // NC
    mine = lax.dynamic_slice_in_dim(out_weight, place[2] * half, half, 0)
    after, before = move(mine, "y", NY, 1), move(mine, "y", NY, -1)
    block = jnp.concatenate([first, move_ring(other)], axis=0)
    block, q2 = lax.optimization_barrier((block, q2))
    state = first_step(place, q2, qpos, own, other)
    kept, entries = [own, other], [(0, False), (0, True)]
    for t in range(1, NZ // 2):
        ahead = move_ring(block if t < NZ // 2 - 1 else block[:COLS])
        other = move(block, "c", NC, 1)
        kept += [block, other]
        entries += [(t, False), (t, True)]
        if t == 1:
            ahead, state = lax.optimization_barrier((ahead, state))
        elif t == 2:
            ahead, state, after, before = lax.optimization_barrier((ahead, state, after, before))
            across = move(after, "y", NY, 1)
        else:
            ahead, state, across = lax.optimization_barrier((ahead, state, across))
            near = jnp.concatenate([after, across, before], axis=0)
            far = move(near, "c", NC, 1)
        state = next_step(place, q2, qpos, block, state, t, False)
        state = next_step(place, q2, qpos, other, state, t, True)
        block = ahead
    t = NZ // 2
    other = move(block, "c", NC, 1)
    kept += [block, other]
    entries += [(t, False), (t, True)]
    state = next_step(place, q2, qpos, block, state, t, False)
    out = last_step(place, q2, qpos, other, state, kept, tuple(entries))
    out = [out[0]] + [move(out[d], "x", NX, -d) for d in range(1, NX)]
    out = [jnp.stack([out[d][e] for d in range(NX)]) for e in range(NY)]
    out = [out[0]] + [move(out[e], "y", NY, e) for e in range(1, NY)]
    here, there = pl.pallas_call(
        project_kernel,
        in_specs=[scalars()] + [whole()] * (NY + 3),
        out_specs=[whole()] * 2,
        out_shape=[jax.ShapeDtypeStruct((ROWS, 1024), BF16)] * 2,
        compiler_params=params(),
        name="project",
    )(place, *out, out_weight, near, far)
    return jnp.concatenate([here, mirror(there)], axis=0)


def solution(mesh):
    split = Mesh(mesh.devices.reshape(NZ, NX, NC, NY), ("z", "x", "c", "y"))
    rows = ("z", "x", "c")
    return jax.shard_map(
        per_device,
        mesh=split,
        in_specs=(P(rows, "y"), P(rows, "y"), P(rows, "y"), P("y", None)),
        out_specs=P((*rows, "y"), None),
        check_vma=False,
    )
```
